128 devices in a mesh: section: 16 (over z_lo, y, core), tensor: 8 (over z_hi, x).
Axes of the slice: x: 4, y: 4, z: 4 (z_hi: 2, z_lo: 2; z = z_hi * 2 + z_lo), core: 2. Of those that a mesh axis runs over, the one named last changes fastest.
Arguments:
- inputs_down: bfloat16 [16, 2, 240, 2048], P('section', None, 'tensor'), may hold values from -6 to 6
- inputs_up: bfloat16 [16, 2, 240, 2048], P('section', None, 'tensor'), may hold values from -6 to 6
- grads_down: bfloat16 [16, 240, 2048], P('section', 'tensor'), may hold values from -6 to 6
- grads_up: bfloat16 [16, 240, 2048], P('section', 'tensor'), may hold values from -6 to 6
- loss_grads: bfloat16 [2, 240, 2048], P(None, 'tensor'), may hold values from -6 to 6
- first_down: bfloat16 [16, 2048, 4096], P('section', None, 'tensor'), may hold values from -6 to 6
- second_down: bfloat16 [16, 4096, 2048], P('section', 'tensor'), may hold values from -6 to 6
- first_up: bfloat16 [16, 2048, 4096], P('section', None, 'tensor'), may hold values from -6 to 6
- second_up: bfloat16 [16, 4096, 2048], P('section', 'tensor'), may hold values from -6 to 6
- momentum_first: bfloat16 [16, 2048, 4096], P('section', None, 'tensor'), may hold values from -3 to 3
- momentum_second: bfloat16 [16, 4096, 2048], P('section', 'tensor'), may hold values from -3 to 3
Outputs:
- first_new: bfloat16 [16, 2048, 4096], P('section', None, 'tensor')
- second_new: bfloat16 [16, 4096, 2048], P('section', 'tensor')
- momentum_one: bfloat16 [16, 2048, 4096], P('section', None, 'tensor')
- momentum_two: bfloat16 [16, 4096, 2048], P('section', 'tensor')
- passed_down: bfloat16 [16, 240, 2048], P('section', 'tensor')
- passed_up: bfloat16 [16, 240, 2048], P('section', 'tensor')
The draws below stay inside these ranges and needn't reach their ends.
All inputs are finite; a program needn't handle non-finite values.
Results may differ from the reference program's by a relative error of at most 0.0063.
Values may be sent and summed in bfloat16 or wider, within the bound.
A program may use at most 128 MiB of HBM per device.

```python
import jax
import jax.numpy as jnp
from jax import lax

D = 2048
FF = 4096
MB_TOK = 240
SECTIONS = 16


def block_levels(own_key, extent, split, low, high):
    factor_of, own = 1.0, jax.random.fold_in(own_key, 6)
    for axis_at, blocks in split:
        heights = jnp.exp(jax.random.uniform(jax.random.fold_in(own, axis_at), (blocks,), jnp.float32, low / len(split), high / len(split)))
        factor_of = factor_of * jnp.repeat(heights, extent[axis_at] // blocks).reshape([-1 if axis == axis_at else 1 for axis in range(len(extent))])
    return factor_of


def normal_values(own_key, dims, width, reach, shards=(), held_as=jnp.bfloat16):
    drawn = width * jax.random.normal(own_key, dims, jnp.float32)
    if shards:
        drawn = drawn * block_levels(own_key, dims, shards, -0.22, 0.18)
    return jnp.clip(drawn, -reach, reach).astype(held_as)


def setup_inputs(seed: int = 0) -> dict:
    splits = jax.random.split(jax.random.key(seed), 12)
    return {
        "inputs_down": normal_values(splits[0], (SECTIONS, 2, MB_TOK, D), 1.0, 6.0, ((0, 16), (2, 8))),
        "inputs_up": normal_values(splits[1], (SECTIONS, 2, MB_TOK, D), 1.0, 6.0, ((0, 16), (2, 8))),
        "grads_down": normal_values(splits[2], (SECTIONS, MB_TOK, D), 1.0, 6.0, ((0, 16), (1, 8))),
        "grads_up": normal_values(splits[3], (SECTIONS, MB_TOK, D), 1.0, 6.0, ((0, 16), (1, 8))),
        "loss_grads": normal_values(splits[4], (2, MB_TOK, D), 1.0, 6.0, ((1, 8),)),
        "first_down": normal_values(splits[5], (SECTIONS, D, FF), 1.0, 6.0, ((0, 16), (2, 8))),
        "second_down": normal_values(splits[6], (SECTIONS, FF, D), 1.0, 6.0, ((0, 16), (1, 8))),
        "first_up": normal_values(splits[7], (SECTIONS, D, FF), 1.0, 6.0, ((0, 16), (2, 8))),
        "second_up": normal_values(splits[8], (SECTIONS, FF, D), 1.0, 6.0, ((0, 16), (1, 8))),
        "momentum_first": normal_values(splits[9], (SECTIONS, D, FF), 0.5, 3.0, ((0, 16), (2, 8))),
        "momentum_second": normal_values(splits[10], (SECTIONS, FF, D), 0.5, 3.0, ((0, 16), (1, 8))),
    }


epsilon = 1e-05
learning_rate = 0.25
momentum_decay = 0.9
tanh_scale = 0.7978845608028654
cubic_term = 0.044715

def gelu_with_slope(preact):
    tanh_input = tanh_scale * (preact + cubic_term * preact * preact * preact)
    tangent = jnp.tanh(tanh_input)
    values = 0.5 * preact * (1.0 + tangent)
    slopes = 0.5 * (1.0 + tangent) + 0.5 * preact * (1.0 - tangent * tangent) * tanh_scale * (1.0 + 3.0 * cubic_term * preact * preact)
    return (values, slopes)

def normalize(inputs):
    widened = inputs.astype(jnp.float32)
    centred = widened - lax.optimization_barrier(jnp.mean(widened, axis=-1, keepdims=True))
    inverse_scale = lax.rsqrt(lax.optimization_barrier(jnp.mean(centred * centred, axis=-1, keepdims=True)) + epsilon)
    return (centred * inverse_scale, inverse_scale)

def contract_rows(left_side, right_side):
    return lax.dot_general(left_side, right_side, (((0,), (0,)), ((), ())), preferred_element_type=jnp.float32)

def contract_last(left_side, right_side):
    return lax.dot_general(left_side, right_side, (((1,), (1,)), ((), ())), preferred_element_type=jnp.float32)

def section_backward(inputs, cotangent, first_weight, second_weight):
    normed, inverse_scale = normalize(inputs)
    normed_low = normed.astype(jnp.bfloat16)
    preact = jnp.dot(normed_low, first_weight, preferred_element_type=jnp.float32) * D ** (-0.5)
    values, slopes = gelu_with_slope(preact)
    activation = values.astype(jnp.bfloat16)
    grad_activation = contract_last(cotangent, second_weight) * FF ** (-0.5)
    grad_preact = (grad_activation * slopes).astype(jnp.bfloat16)
    grad_normed = contract_last(grad_preact, first_weight) * D ** (-0.5)
    first_mean = lax.optimization_barrier(jnp.mean(grad_normed, axis=-1, keepdims=True))
    second_mean = lax.optimization_barrier(jnp.mean(grad_normed * normed, axis=-1, keepdims=True))
    grad_inputs = cotangent.astype(jnp.float32) + inverse_scale * (grad_normed - first_mean - normed * second_mean)
    grad_first = contract_rows(normed_low, grad_preact) * D ** (-0.5)
    grad_second = contract_rows(activation, cotangent) * FF ** (-0.5)
    return (grad_inputs.astype(jnp.bfloat16), (grad_first, grad_second))

def reference(inputs_down, inputs_up, grads_down, grads_up, loss_grads, first_down, second_down, first_up, second_up, momentum_first, momentum_second):
    weights = (first_down, second_down, first_up, second_up)

    def step_one(packed):
        passed_down, down_grads = section_backward(packed[0][0], packed[2], packed[4], packed[5])
        passed_up, up_grads = section_backward(packed[1][0], packed[3], packed[6], packed[7])
        return (passed_down, passed_up, down_grads, up_grads)
    one_down, one_up, down_one, up_one = lax.map(step_one, (inputs_down, inputs_up, grads_down, grads_up) + weights)
    cotan_down = jnp.concatenate([one_down[1:], loss_grads[0:1]], axis=0)
    cotan_up = jnp.concatenate([loss_grads[1:2], one_up[:-1]], axis=0)

    def step_two(packed):
        passed_down, down_grads = section_backward(packed[0][1], packed[2], packed[4], packed[5])
        passed_up, up_grads = section_backward(packed[1][1], packed[3], packed[6], packed[7])
        down_sums = (down_grads[0] + packed[8][0], down_grads[1] + packed[8][1])
        up_sums = ((up_grads[0] + packed[9][0]).astype(jnp.bfloat16), (up_grads[1] + packed[9][1]).astype(jnp.bfloat16))
        return (passed_down, passed_up, down_sums, up_sums)
    passed_down, passed_up, down_sums, up_sums = lax.map(step_two, (inputs_down, inputs_up, cotan_down, cotan_up) + weights + (down_one, up_one))
    total_first = down_sums[0] + up_sums[0][::-1].astype(jnp.float32)
    total_second = down_sums[1] + up_sums[1][::-1].astype(jnp.float32)
    moment_first = momentum_decay * momentum_first.astype(jnp.float32) + total_first
    moment_second = momentum_decay * momentum_second.astype(jnp.float32) + total_second
    first_new = (first_down.astype(jnp.float32) - learning_rate * moment_first).astype(jnp.bfloat16)
    second_new = (second_down.astype(jnp.float32) - learning_rate * moment_second).astype(jnp.bfloat16)
    return (first_new, second_new, moment_first.astype(jnp.bfloat16), moment_second.astype(jnp.bfloat16), passed_down, passed_up)
```

```python
import functools

import jax
import jax.numpy as jnp
from jax import lax
from jax.experimental import pallas as pl
from jax.experimental.pallas import tpu as pltpu
from jax.sharding import PartitionSpec as P

D = 2048
FF = 4096
ROWS = 30
PAD = 32
HID = 512
TILE = 256
OPCOLS = 1024
MESH = pl.DeviceIdType.MESH

epsilon = 1e-05
learning_rate = 0.25
momentum_decay = 0.9
tanh_scale = 0.7978845608028654
cubic_term = 0.044715

N1U, C1U, N2U, C2U, N1D, C1D, N2D, C2D = range(8)
U1, U2, D1, D2 = range(4)
NT = D // TILE
NOP = OPCOLS // TILE
NGR = NT - NOP


def gelu_with_slope(preact):
    tanh_input = tanh_scale * (preact + cubic_term * preact * preact * preact)
    tangent = jnp.tanh(tanh_input)
    values = 0.5 * preact * (1.0 + tangent)
    slopes = 0.5 * (1.0 + tangent) + 0.5 * preact * (1.0 - tangent * tangent) * tanh_scale * (
        1.0 + 3.0 * cubic_term * preact * preact
    )
    return (values, slopes)


def dot_nt(a, b):
    return lax.dot_general(a, b, (((1,), (1,)), ((), ())), preferred_element_type=jnp.float32)


def dot_tn(a, b):
    return lax.dot_general(a, b, (((0,), (0,)), ((), ())), preferred_element_type=jnp.float32)


def kernel(
    in_down, in_up, g_down, g_up, loss,
    w1d_h, w2d_h, w1u_h, w2u_h, m1_h, m2_h,
    f_new, s_new, mo1, mo2, pass_d, pass_u,
    G, W1, W2, M1, M2, A, GP, PB, RR, ZB, NR, SC, CT, RL,
    MO, MG, MA, SF, SS, RF, RS,
    load_sem, out_sem, ag_s, ag_r, rs_s, rs_r, rl_s, rl_r, mo_s, mo_r, mg_s, mg_r, ma_s, ma_r,
    sf_s, sf_r, ss_s, ss_r,
):
    s = lax.axis_index("section")
    t = lax.axis_index("tensor")
    x = lax.rem(t, 4)
    zh = t // 4
    zo = 1 - zh

    def xpeer(k):
        return (s, zh * 4 + lax.rem(x + k, 4))

    zpeer = (s, zo * 4 + x)
    mirror = (15 - s, t)
    up = (lax.rem(s + 1, 16), t)
    down = (lax.rem(s + 15, 16), t)

    barrier = pltpu.get_barrier_semaphore()
    for peer in (xpeer(1), xpeer(2), xpeer(3), zpeer, mirror, up, down):
        pl.semaphore_signal(barrier, inc=1, device_id=peer, device_id_type=MESH)

    loads = []
    for i, (src, dst) in enumerate(
        ((w1u_h, W1.at[0]), (w2u_h, W2.at[0]), (w1d_h, W1.at[1]), (w2d_h, W2.at[1]), (m1_h, M1), (m2_h, M2))
    ):
        c = pltpu.make_async_copy(src.at[0], dst, load_sem.at[i])
        c.start()
        loads.append(c)

    def put_normed(ref, step, q, a):
        wide = ref[0, step].astype(jnp.float32)
        centred = wide - jnp.mean(wide, axis=-1, keepdims=True)
        inv = lax.rsqrt(jnp.mean(centred * centred, axis=-1, keepdims=True) + epsilon)
        NR[q, ROWS:PAD] = jnp.zeros((PAD - ROWS, D), jnp.float32)
        NR[q, 0:ROWS] = centred * inv
        SC[q, ROWS:PAD] = jnp.zeros((PAD - ROWS, 128), jnp.float32)
        SC[q, 0:ROWS] = jnp.broadcast_to(inv, (ROWS, 128))
        G[a, t] = NR[q].astype(jnp.bfloat16)

    def put_rows(value, a):
        CT[ROWS:PAD] = jnp.zeros((PAD - ROWS, D), jnp.float32)
        CT[0:ROWS] = value.astype(jnp.float32)
        G[a, t] = CT[...].astype(jnp.bfloat16)

    def rcopy(src, dst, ss, rs, dev):
        return pltpu.make_async_remote_copy(
            src_ref=src, dst_ref=dst, send_sem=ss, recv_sem=rs, device_id=dev, device_id_type=MESH
        )

    pending = []

    def send(src, dst, ss, rs, dev):
        c = rcopy(src, dst, ss, rs, dev)
        c.start()
        pending.append(c)

    def slot_send(a, slot, i, dev):
        send(G.at[a, slot], G.at[a, slot], ag_s.at[a, i], ag_r.at[a, i], dev)

    def slot_wait(a, slot, i):
        rcopy(G.at[a, slot], G.at[a, slot], ag_s.at[a, i], ag_r.at[a, i], zpeer).wait_recv()

    def from_x(k):
        return lax.rem(x + 4 - k, 4)

    def ag_z(a):
        slot_send(a, t, 0, zpeer)

    def ag_x(a):
        for k in (1, 3, 2):
            slot_send(a, t, k, xpeer(k))

    def ag_fwd(a):
        slot_wait(a, zo * 4 + x, 0)
        for k in (1, 3, 2):
            slot_send(a, zo * 4 + x, 4 + k, xpeer(k))

    def ag_wait(a):
        for k in (1, 3, 2):
            slot_wait(a, zh * 4 + from_x(k), k)
        for k in (1, 3, 2):
            slot_wait(a, zo * 4 + from_x(k), 4 + k)

    def ag_fwd_xf(a):
        for k in (1, 3, 2):
            slot_wait(a, zh * 4 + from_x(k), k)
            slot_send(a, zh * 4 + from_x(k), 4 + k, zpeer)

    def ag_wait_xf(a):
        slot_wait(a, zo * 4 + x, 0)
        for k in (1, 3, 2):
            slot_wait(a, zo * 4 + from_x(k), 4 + k)

    def hidden(q, w, an, ac):
        @pl.loop(0, HID // TILE)
        def _(j):
            cols = pl.ds(pl.multiple_of(j * TILE, TILE), TILE)
            n = G[an].reshape(8 * PAD, D)
            pre = jnp.dot(n, W1[w, :, cols], preferred_element_type=jnp.float32) * D ** (-0.5)
            values, slopes = gelu_with_slope(pre)
            A[q, :, cols] = values.astype(jnp.bfloat16)
            c = G[ac].reshape(8 * PAD, D)
            ga = dot_nt(c, W2[w, cols, :]) * FF ** (-0.5)
            GP[q, :, cols] = (ga * slopes).astype(jnp.bfloat16)

    def partial(q, w):
        @pl.loop(0, NT)
        def _(j):
            cols = pl.ds(pl.multiple_of(j * TILE, TILE), TILE)
            part = dot_nt(GP[q], W1[w, cols, :]) * D ** (-0.5)
            PB[q, :, :, cols] = part.astype(jnp.bfloat16).reshape(8, PAD, TILE)

    def rs_start(q):
        for k in (2, 1, 3):
            xk = lax.rem(x + k, 4)
            send(PB.at[q, zo * 4 + xk], RR.at[q, 4 + k], rs_s.at[q, 4 + k], rs_r.at[q, 4 + k], xpeer(k))
        for k in (2, 1, 3):
            xk = lax.rem(x + k, 4)
            send(PB.at[q, zh * 4 + xk], RR.at[q, k], rs_s.at[q, k], rs_r.at[q, k], xpeer(k))

    def rs_wait(q, i):
        rcopy(RR.at[q, i], RR.at[q, i], rs_s.at[q, i], rs_r.at[q, i], zpeer).wait_recv()

    def rs_mid(q):
        for k in (1, 3, 2):
            rs_wait(q, 4 + k)
        total = PB[q, zo * 4 + x].astype(jnp.float32)
        for k in (1, 2, 3):
            total = total + RR[q, 4 + k].astype(jnp.float32)
        ZB[q] = total.astype(jnp.bfloat16)
        send(ZB.at[q], RR.at[q, 0], rs_s.at[q, 0], rs_r.at[q, 0], zpeer)

    def rs_end(q, ac):
        for k in (1, 3, 2):
            rs_wait(q, k)
        total = PB[q, t].astype(jnp.float32)
        for k in (1, 2, 3):
            total = total + RR[q, k].astype(jnp.float32)
        rs_wait(q, 0)
        gn = total + RR[q, 0].astype(jnp.float32)
        normed = NR[q]
        first_mean = jnp.mean(gn, axis=-1, keepdims=True)
        second_mean = jnp.mean(gn * normed, axis=-1, keepdims=True)
        return G[ac, t].astype(jnp.float32) + SC[q, :, 0:1] * (gn - first_mean - normed * second_mean)

    def relay(q, ac, i, a, dev):
        RL[i] = rs_end(q, ac).astype(jnp.bfloat16)
        send(RL.at[i], G.at[a, t], rl_s.at[i], rl_r.at[i], dev)

    def relay_wait(i, a, edge, row):
        rcopy(RL.at[i], G.at[a, t], rl_s.at[i], rl_r.at[i], zpeer).wait_recv()

        @pl.when(s == edge)
        def _():
            put_rows(loss[row], a)

    def mirror_cols(a):
        send(G.at[a, :, :, 0:OPCOLS], MO.at[a], mo_s.at[a], mo_r.at[a], mirror)

    def mirror_hidden(q):
        send(GP.at[q], MG.at[q], mg_s.at[q], mg_r.at[q], mirror)
        send(A.at[q], MA.at[q], ma_s.at[q], ma_r.at[q], mirror)

    def flat(ref, a, cols):
        return ref[a, :, :, cols].reshape(8 * PAD, TILE)

    put_rows(g_up[0], C1U)
    put_normed(in_up, 0, U1, N1U)
    pl.semaphore_wait(barrier, 7)
    ag_z(C1U)
    ag_x(N1U)
    ag_x(C1U)
    ag_z(N1U)
    put_normed(in_up, 1, U2, N2U)
    put_normed(in_down, 0, D1, N1D)
    put_rows(g_down[0], C1D)
    put_normed(in_down, 1, D2, N2D)
    ag_fwd(C1U)
    ag_fwd_xf(N1U)
    ag_z(N2U)
    loads[0].wait()
    loads[1].wait()
    ag_wait(C1U)
    ag_wait_xf(N1U)
    ag_z(N1D)
    ag_z(C1D)
    mirror_cols(C1U)
    mirror_cols(N1U)
    ag_x(N2U)
    ag_fwd(N2U)
    hidden(U1, 0, N1U, C1U)
    partial(U1, 0)
    rs_start(U1)
    mirror_hidden(U1)
    ag_z(N2D)
    ag_wait(N2U)
    mirror_cols(N2U)
    rs_mid(U1)
    ag_x(N1D)
    relay(U1, C1U, 0, C2U, up)
    ag_fwd(N1D)
    relay_wait(0, C2U, 0, 1)
    ag_z(C2U)
    ag_x(C2U)
    ag_x(C1D)
    ag_fwd(C2U)
    ag_fwd(C1D)
    loads[2].wait()
    loads[3].wait()
    ag_wait(C2U)
    hidden(U2, 0, N2U, C2U)
    mirror_hidden(U2)
    mirror_cols(C2U)

    for j in range(NGR):
        cols = pl.ds(OPCOLS + j * TILE, TILE)
        gf = dot_tn(flat(G, N1U, cols), GP[U1]) + dot_tn(flat(G, N2U, cols), GP[U2])
        SF[j] = (gf * D ** (-0.5)).astype(jnp.bfloat16)
        send(SF.at[j], RF.at[j], sf_s.at[j], sf_r.at[j], mirror)
        gs = dot_tn(A[U1], flat(G, C1U, cols)) + dot_tn(A[U2], flat(G, C2U, cols))
        SS[j] = (gs * FF ** (-0.5)).astype(jnp.bfloat16)
        send(SS.at[j], RS.at[j], ss_s.at[j], ss_r.at[j], mirror)

    ag_wait(N1D)
    ag_wait(C1D)
    hidden(D1, 1, N1D, C1D)
    partial(D1, 1)
    rs_start(D1)
    ag_x(N2D)
    ag_fwd(N2D)
    partial(U2, 0)
    rs_mid(D1)
    relay(D1, C1D, 1, C2D, down)
    rs_start(U2)
    relay_wait(1, C2D, 15, 0)
    ag_z(C2D)
    ag_x(C2D)
    ag_fwd(C2D)
    rs_mid(U2)
    ag_wait(N2D)
    ag_wait(C2D)
    hidden(D2, 1, N2D, C2D)
    partial(D2, 1)
    rs_start(D2)

    CT[...] = rs_end(U2, C2U)
    pass_u[0] = CT[0:ROWS].astype(jnp.bfloat16)

    loads[4].wait()
    loads[5].wait()
    outs = []

    def update(j, first_mirror, second_mirror):
        cols = pl.ds(j * TILE, TILE)
        gf = dot_tn(flat(G, N1D, cols), GP[D1]) + dot_tn(flat(G, N2D, cols), GP[D2])
        moment = momentum_decay * M1[cols, :].astype(jnp.float32) + gf * D ** (-0.5) + first_mirror()
        M1[cols, :] = moment.astype(jnp.bfloat16)
        W1[1, cols, :] = (W1[1, cols, :].astype(jnp.float32) - learning_rate * moment).astype(jnp.bfloat16)
        gs = dot_tn(A[D1], flat(G, C1D, cols)) + dot_tn(A[D2], flat(G, C2D, cols))
        moment = momentum_decay * M2[:, cols].astype(jnp.float32) + gs * FF ** (-0.5) + second_mirror()
        M2[:, cols] = moment.astype(jnp.bfloat16)
        W2[1, :, cols] = (W2[1, :, cols].astype(jnp.float32) - learning_rate * moment).astype(jnp.bfloat16)
        for i, (src, dst) in enumerate((
            (W1.at[1, cols, :], f_new.at[0, cols, :]),
            (M1.at[cols, :], mo1.at[0, cols, :]),
            (W2.at[1, :, cols], s_new.at[0, :, cols]),
            (M2.at[:, cols], mo2.at[0, :, cols]),
        )):
            c = pltpu.make_async_copy(src, dst, out_sem.at[j, i])
            c.start()
            outs.append(c)

    for q in (U1, U2):
        rcopy(GP.at[q], MG.at[q], mg_s.at[q], mg_r.at[q], mirror).wait_recv()
        rcopy(A.at[q], MA.at[q], ma_s.at[q], ma_r.at[q], mirror).wait_recv()
    for a in (N1U, C1U, N2U, C2U):
        rcopy(MO.at[a], MO.at[a], mo_s.at[a], mo_r.at[a], mirror).wait_recv()
    for j in range(NOP):
        cols = pl.ds(j * TILE, TILE)
        update(
            j,
            lambda: (dot_tn(flat(MO, N1U, cols), MG[U1]) + dot_tn(flat(MO, N2U, cols), MG[U2])) * D ** (-0.5),
            lambda: (dot_tn(MA[U1], flat(MO, C1U, cols)) + dot_tn(MA[U2], flat(MO, C2U, cols))) * FF ** (-0.5),
        )
    rs_mid(D2)
    for j in range(NGR):
        rcopy(SF.at[j], RF.at[j], sf_s.at[j], sf_r.at[j], mirror).wait_recv()
        rcopy(SS.at[j], RS.at[j], ss_s.at[j], ss_r.at[j], mirror).wait_recv()
        update(
            NOP + j,
            lambda: RF[j].astype(jnp.float32),
            lambda: RS[j].astype(jnp.float32),
        )
    CT[...] = rs_end(D2, C2D)
    pass_d[0] = CT[0:ROWS].astype(jnp.bfloat16)
    for c in pending:
        c.wait_send()
    for c in outs:
        c.wait()


def body(*blocks):
    bf16, f32 = jnp.bfloat16, jnp.float32
    dma = pltpu.SemaphoreType.DMA
    vmem = pl.BlockSpec(memory_space=pltpu.VMEM)
    hbm = pl.BlockSpec(memory_space=pl.ANY)
    return pl.pallas_call(
        kernel,
        out_shape=(
            jax.ShapeDtypeStruct((1, D, HID), bf16),
            jax.ShapeDtypeStruct((1, HID, D), bf16),
            jax.ShapeDtypeStruct((1, D, HID), bf16),
            jax.ShapeDtypeStruct((1, HID, D), bf16),
            jax.ShapeDtypeStruct((1, ROWS, D), bf16),
            jax.ShapeDtypeStruct((1, ROWS, D), bf16),
        ),
        in_specs=[vmem] * 5 + [hbm] * 6,
        out_specs=[hbm] * 4 + [vmem] * 2,
        scratch_shapes=[
            pltpu.VMEM((8, 8, PAD, D), bf16),
            pltpu.VMEM((2, D, HID), bf16),
            pltpu.VMEM((2, HID, D), bf16),
            pltpu.VMEM((D, HID), bf16),
            pltpu.VMEM((HID, D), bf16),
            pltpu.VMEM((4, 8 * PAD, HID), bf16),
            pltpu.VMEM((4, 8 * PAD, HID), bf16),
            pltpu.VMEM((4, 8, PAD, D), bf16),
            pltpu.VMEM((4, 8, PAD, D), bf16),
            pltpu.VMEM((4, PAD, D), bf16),
            pltpu.VMEM((4, PAD, D), f32),
            pltpu.VMEM((4, PAD, 128), f32),
            pltpu.VMEM((PAD, D), f32),
            pltpu.VMEM((2, PAD, D), bf16),
            pltpu.VMEM((4, 8, PAD, OPCOLS), bf16),
            pltpu.VMEM((2, 8 * PAD, HID), bf16),
            pltpu.VMEM((2, 8 * PAD, HID), bf16),
            pltpu.VMEM((NGR, TILE, HID), bf16),
            pltpu.VMEM((NGR, HID, TILE), bf16),
            pltpu.VMEM((NGR, TILE, HID), bf16),
            pltpu.VMEM((NGR, HID, TILE), bf16),
            dma((6,)), dma((NT, 4)),
            dma((8, 8)), dma((8, 8)),
            dma((4, 8)), dma((4, 8)),
            dma((2,)), dma((2,)),
            dma((4,)), dma((4,)),
            dma((2,)), dma((2,)), dma((2,)), dma((2,)),
            dma((NGR,)), dma((NGR,)), dma((NGR,)), dma((NGR,)),
        ],
        compiler_params=pltpu.CompilerParams(
            collective_id=0, has_side_effects=True, vmem_limit_bytes=60 * 2**20
        ),
        cost_estimate=pl.CostEstimate(flops=12 * 10**9, bytes_accessed=21 * 10**6, transcendentals=10**6),
        name="relay_backward",
    )(*blocks)


def solution(mesh):
    placed = (
        P("section", None, "tensor", None),
        P("section", None, "tensor", None),
        P("section", "tensor", None),
        P("section", "tensor", None),
        P(None, "tensor", None),
        P("section", None, "tensor"),
        P("section", "tensor", None),
        P("section", None, "tensor"),
        P("section", "tensor", None),
        P("section", None, "tensor"),
        P("section", "tensor", None),
    )
    return jax.shard_map(
        body,
        mesh=mesh,
        in_specs=placed,
        out_specs=(
            P("section", None, "tensor"),
            P("section", "tensor", None),
            P("section", None, "tensor"),
            P("section", "tensor", None),
            P("section", "tensor", None),
            P("section", "tensor", None),
        ),
        check_vma=False,
    )
```

```python
import functools

import jax
import jax.numpy as jnp
from jax import lax
from jax.experimental import pallas as pl
from jax.experimental.pallas import tpu as pltpu
from jax.sharding import PartitionSpec as P

D = 2048
FF = 4096
ROWS = 30
PAD = 32
HID = 512
TILE = 256
MESH = pl.DeviceIdType.MESH

epsilon = 1e-05
learning_rate = 0.25
momentum_decay = 0.9
tanh_scale = 0.7978845608028654
cubic_term = 0.044715

N1U, C1U, N2U, C2U, N1D, C1D, N2D, C2D, N1M, C1M, N2M, C2M = range(12)
U1, U2, D1, D2 = range(4)
NT = D // TILE
HALF = PAD // 2
MODES = (0, 0, 0, 0, 0, 1, 1, 1, 1, 0, 0, 1)
ORDER = (
    (0, N1D), (0, C1D), (0, N2U), (1, N1D), (1, C1D), (0, N1M), (2, N1D), (2, C1D), (1, N2U), (0, N2D), (1, N1M),
    (2, N2U), (0, C1M), (0, C2M), (0, N2M), (1, C1M), (1, N2M), (1, N2D), (2, N1M), (2, C1M), (2, N2M), (2, N2D),
    (1, C2M), (2, C2M),
)
FILLS = (2, 1, 0, 2, 3, 2, 2, 3, 0, 3, 1, 3, 0, 1, 0, 25, 20)


def gelu_with_slope(preact):
    tanh_input = tanh_scale * (preact + cubic_term * preact * preact * preact)
    tangent = jnp.tanh(tanh_input)
    values = 0.5 * preact * (1.0 + tangent)
    slopes = 0.5 * (1.0 + tangent) + 0.5 * preact * (1.0 - tangent * tangent) * tanh_scale * (
        1.0 + 3.0 * cubic_term * preact * preact
    )
    return (values, slopes)


def dot_nt(a, b):
    return lax.dot_general(a, b, (((1,), (1,)), ((), ())), preferred_element_type=jnp.float32)


def dot_tn(a, b):
    return lax.dot_general(a, b, (((0,), (0,)), ((), ())), preferred_element_type=jnp.float32)


def kernel(
    in_down, in_up, g_down, g_up, loss, w1d_h, w2d_h, w1u_h, w2u_h,
    t1_h, t2_h, pass_d, pass_u,
    G, W1, W2, A, GP, PB, RR, ZB, NR, SC, CT, RL, MG, MA, ACC1, ACC2, T1, T2,
    load_sem, out_sem, ag_s, ag_r, rs_s, rs_r, rl_s, rl_r, row_s, row_r, mg_s, mg_r, ma_s, ma_r,
):
    s = lax.axis_index("section")
    t = lax.axis_index("tensor")
    x = lax.rem(t, 4)
    zh = t // 4
    zo = 1 - zh

    def xpeer(k):
        return (s, zh * 4 + lax.rem(x + k, 4))

    zpeer = (s, zo * 4 + x)
    mirror = (15 - s, t)
    up = (lax.rem(s + 1, 16), t)
    down = (lax.rem(s + 15, 16), t)

    barrier = pltpu.get_barrier_semaphore()
    for peer in (xpeer(1), xpeer(2), xpeer(3), zpeer, mirror, up, down):
        pl.semaphore_signal(barrier, inc=1, device_id=peer, device_id_type=MESH)

    loads = []
    for i, (src, dst) in enumerate(
        ((w1u_h, W1.at[0]), (w2u_h, W2.at[0]), (w1d_h, W1.at[1]), (w2d_h, W2.at[1]))
    ):
        c = pltpu.make_async_copy(src.at[0], dst, load_sem.at[i])
        c.start()
        loads.append(c)

    def put_normed(ref, step, q, a):
        wide = ref[0, step].astype(jnp.float32)
        centred = wide - jnp.mean(wide, axis=-1, keepdims=True)
        inv = lax.rsqrt(jnp.mean(centred * centred, axis=-1, keepdims=True) + epsilon)
        NR[q, ROWS:PAD] = jnp.zeros((PAD - ROWS, D), jnp.float32)
        NR[q, 0:ROWS] = centred * inv
        SC[q, ROWS:PAD] = jnp.zeros((PAD - ROWS, 128), jnp.float32)
        SC[q, 0:ROWS] = jnp.broadcast_to(inv, (ROWS, 128))
        G[a, t] = NR[q].astype(jnp.bfloat16)

    def put_rows(value, a):
        CT[ROWS:PAD] = jnp.zeros((PAD - ROWS, D), jnp.float32)
        CT[0:ROWS] = value.astype(jnp.float32)
        G[a, t] = CT[...].astype(jnp.bfloat16)

    def rcopy(src, dst, ss, rs, dev):
        return pltpu.make_async_remote_copy(
            src_ref=src, dst_ref=dst, send_sem=ss, recv_sem=rs, device_id=dev, device_id_type=MESH
        )

    pending = []

    def send(src, dst, ss, rs, dev):
        c = rcopy(src, dst, ss, rs, dev)
        c.start()
        pending.append(c)

    waited = set()

    def ag_ref(a, slot, half=None):
        return G.at[a, slot] if half is None else G.at[a, slot, pl.ds(half * HALF, HALF)]

    def ag_send(a, i, dev, slot, half=None):
        ref = ag_ref(a, slot, half)
        send(ref, ref, ag_s.at[a, i], ag_r.at[a, i], dev)

    def near(k):
        return zh * 4 + lax.rem(x + k, 4)

    def far(k):
        return zo * 4 + lax.rem(x + k, 4)

    def landing(a, i):
        first = MODES[a] == 0
        return (
            (far(0), None), (near(3), None), (near(1), None), (near(2), 0), (near(2), 1),
            (far(3), None), (far(1), None),
            (far(2), 0 if first else None), (far(2), 1),
        )[i]

    def ag_wait(a, *which):
        for i in which:
            if (a, i) not in waited:
                waited.add((a, i))
                ref = ag_ref(a, *landing(a, i))
                rcopy(ref, ref, ag_s.at[a, i], ag_r.at[a, i], zpeer).wait_recv()

    def ag_done(a):
        ag_wait(a, *range(9 if MODES[a] == 0 else 8))

    def row_wait(i):
        ref = G.at[N1M + i, t]
        rcopy(ref, ref, row_s.at[i], row_r.at[i], mirror).wait_recv()

    def stage(a, k):
        first = MODES[a] == 0
        if k == 0:
            if a >= N1M:
                row_wait(a - N1M)
            if first:
                ag_send(a, 0, zpeer, t)
            ag_send(a, 1, xpeer(1), t)
            ag_send(a, 2, xpeer(3), t)
            if not first:
                ag_send(a, 0, zpeer, t)
        elif k == 1:
            ag_wait(a, 1)
            ag_send(a, 3, xpeer(1), near(3), 0)
            if not first:
                ag_send(a, 5, zpeer, near(3))
            ag_wait(a, 2)
            ag_send(a, 4, xpeer(3), near(1), 1)
            if not first:
                ag_send(a, 6, zpeer, near(1))
            else:
                ag_wait(a, 0)
                ag_send(a, 5, xpeer(1), far(0))
                ag_send(a, 6, xpeer(3), far(0))
        elif first:
            ag_wait(a, 5)
            ag_send(a, 7, xpeer(1), far(3), 0)
            ag_wait(a, 6)
            ag_send(a, 8, xpeer(3), far(1), 1)
        else:
            ag_wait(a, 3, 4)
            ag_send(a, 7, zpeer, near(2))

    def row(a):
        send(G.at[a, t], G.at[N1M + a, t], row_s.at[a], row_r.at[a], mirror)

    queue = list(ORDER)
    fills = list(FILLS)
    ready = {N1M, C1M, N2M}

    def run_next():
        k, a = queue.pop(0)
        stage(a, k)

    def fill():
        for _ in range(fills.pop(0)):
            if queue and (queue[0][1] < N1M or queue[0][1] in ready):
                run_next()

    def need(*arrays):
        while any(a in arrays for _, a in queue):
            run_next()
        for a in arrays:
            ag_done(a)

    def hidden(q, w, an, ac):
        @pl.loop(0, HID // TILE)
        def _(j):
            cols = pl.ds(pl.multiple_of(j * TILE, TILE), TILE)
            n = G[an].reshape(8 * PAD, D)
            pre = jnp.dot(n, W1[w, :, cols], preferred_element_type=jnp.float32) * D ** (-0.5)
            values, slopes = gelu_with_slope(pre)
            A[q, :, cols] = values.astype(jnp.bfloat16)
            c = G[ac].reshape(8 * PAD, D)
            ga = dot_nt(c, W2[w, cols, :]) * FF ** (-0.5)
            GP[q, :, cols] = (ga * slopes).astype(jnp.bfloat16)

    def partial(q, w):
        @pl.loop(0, NT)
        def _(j):
            cols = pl.ds(pl.multiple_of(j * TILE, TILE), TILE)
            part = dot_nt(GP[q], W1[w, cols, :]) * D ** (-0.5)
            PB[q, :, :, cols] = part.astype(jnp.bfloat16).reshape(8, PAD, TILE)

    def rs_start(q):
        for k in (2, 1, 3):
            send(PB.at[q, far(k)], RR.at[q, 4 + k], rs_s.at[q, 4 + k], rs_r.at[q, 4 + k], xpeer(k))
        for k in (2, 1, 3):
            send(PB.at[q, near(k)], RR.at[q, k], rs_s.at[q, k], rs_r.at[q, k], xpeer(k))

    def rs_wait(q, i):
        rcopy(RR.at[q, i], RR.at[q, i], rs_s.at[q, i], rs_r.at[q, i], zpeer).wait_recv()

    def rs_mid(q):
        for k in (1, 3, 2):
            rs_wait(q, 4 + k)
        total = PB[q, far(0)].astype(jnp.float32)
        for k in (1, 2, 3):
            total = total + RR[q, 4 + k].astype(jnp.float32)
        ZB[q] = total.astype(jnp.bfloat16)
        send(ZB.at[q], RR.at[q, 0], rs_s.at[q, 0], rs_r.at[q, 0], zpeer)

    def rs_end(q, ac):
        for k in (1, 3, 2):
            rs_wait(q, k)
        total = PB[q, t].astype(jnp.float32)
        for k in (1, 2, 3):
            total = total + RR[q, k].astype(jnp.float32)
        rs_wait(q, 0)
        gn = total + RR[q, 0].astype(jnp.float32)
        normed = NR[q]
        first_mean = jnp.mean(gn, axis=-1, keepdims=True)
        second_mean = jnp.mean(gn * normed, axis=-1, keepdims=True)
        return G[ac, t].astype(jnp.float32) + SC[q, :, 0:1] * (gn - first_mean - normed * second_mean)

    def relay(q, ac, i, a, dev):
        RL[i] = rs_end(q, ac).astype(jnp.bfloat16)
        send(RL.at[i], G.at[a, t], rl_s.at[i], rl_r.at[i], dev)

    def relay_wait(i, a, edge, which):
        rcopy(RL.at[i], G.at[a, t], rl_s.at[i], rl_r.at[i], zpeer).wait_recv()

        @pl.when(s == edge)
        def _():
            put_rows(loss[which], a)

    def mirror_hidden(q):
        send(GP.at[q], MG.at[q], mg_s.at[q], mg_r.at[q], mirror)
        send(A.at[q], MA.at[q], ma_s.at[q], ma_r.at[q], mirror)

    def mirror_wait(q):
        rcopy(GP.at[q], MG.at[q], mg_s.at[q], mg_r.at[q], mirror).wait_recv()
        rcopy(A.at[q], MA.at[q], ma_s.at[q], ma_r.at[q], mirror).wait_recv()

    def flat(a, cols):
        return G[a, :, :, cols].reshape(8 * PAD, TILE)

    def out_copies(j):
        cols = pl.ds(pl.multiple_of(j * TILE, TILE), TILE)
        return (
            pltpu.make_async_copy(T1.at[cols, :], t1_h.at[cols, :], out_sem.at[0, j]),
            pltpu.make_async_copy(T2.at[:, cols], t2_h.at[:, cols], out_sem.at[1, j]),
        )

    def add_terms(terms, first=False, last=False):
        @pl.loop(0, NT)
        def _(j):
            cols = pl.ds(pl.multiple_of(j * TILE, TILE), TILE)
            one = sum(dot_tn(flat(n, cols), gp[q]) for n, c, gp, ac, q in terms)
            two = sum(dot_tn(ac[q], flat(c, cols)) for n, c, gp, ac, q in terms)
            if not first:
                one = one + ACC1[cols, :]
                two = two + ACC2[:, cols]
            if last:
                T1[cols, :] = (one * D ** (-0.5)).astype(jnp.bfloat16)
                T2[:, cols] = (two * FF ** (-0.5)).astype(jnp.bfloat16)
                for c in out_copies(j):
                    c.start()
            else:
                ACC1[cols, :] = one
                ACC2[:, cols] = two

    put_rows(g_up[0], C1U)
    put_normed(in_up, 0, U1, N1U)
    pl.semaphore_wait(barrier, 7)
    row(C1U)
    row(N1U)
    stage(N1U, 0)
    stage(C1U, 0)
    put_normed(in_down, 0, D1, N1D)
    put_rows(g_down[0], C1D)
    put_normed(in_up, 1, U2, N2U)
    put_normed(in_down, 1, D2, N2D)
    row(N2U)
    stage(N1U, 1)
    stage(C1U, 1)
    stage(N1U, 2)
    stage(C1U, 2)
    fill()
    loads[0].wait()
    loads[1].wait()
    ag_done(N1U)
    ag_done(C1U)
    fill()
    hidden(U1, 0, N1U, C1U)
    partial(U1, 0)
    rs_start(U1)
    mirror_hidden(U1)
    fill()
    rs_mid(U1)
    fill()
    relay(U1, C1U, 0, C2U, up)
    fill()
    relay_wait(0, C2U, 0, 1)
    stage(C2U, 0)
    row(C2U)
    ready.add(C2M)
    fill()
    stage(C2U, 1)
    fill()
    stage(C2U, 2)
    fill()
    need(N2U)
    ag_done(C2U)
    hidden(U2, 0, N2U, C2U)
    mirror_hidden(U2)
    need(N1D, C1D)
    loads[2].wait()
    loads[3].wait()
    hidden(D1, 1, N1D, C1D)
    partial(D1, 1)
    rs_start(D1)
    fill()
    partial(U2, 0)
    add_terms([(N1D, C1D, GP, A, D1)], first=True)
    rs_mid(D1)
    fill()
    relay(D1, C1D, 1, C2D, down)
    fill()
    relay_wait(1, C2D, 15, 0)
    stage(C2D, 0)
    fill()
    stage(C2D, 1)
    fill()
    rs_start(U2)
    stage(C2D, 2)
    fill()
    need(N2D)
    ag_done(C2D)
    hidden(D2, 1, N2D, C2D)
    partial(D2, 1)
    rs_start(D2)
    fill()
    rs_mid(U2)
    fill()
    need(N1M, C1M)
    mirror_wait(U1)
    add_terms([(N2D, C2D, GP, A, D2), (N1M, C1M, MG, MA, U1)])
    CT[...] = rs_end(U2, C2U)
    pass_u[0] = CT[0:ROWS].astype(jnp.bfloat16)
    rs_mid(D2)
    need(N2M, C2M)
    mirror_wait(U2)
    add_terms([(N2M, C2M, MG, MA, U2)], last=True)
    CT[...] = rs_end(D2, C2D)
    pass_d[0] = CT[0:ROWS].astype(jnp.bfloat16)
    for c in pending:
        c.wait_send()

    @pl.loop(0, NT)
    def _(j):
        for c in out_copies(j):
            c.wait()


def backward(*blocks):
    bf16, f32 = jnp.bfloat16, jnp.float32
    dma = pltpu.SemaphoreType.DMA
    vmem = pl.BlockSpec(memory_space=pltpu.VMEM)
    hbm = pl.BlockSpec(memory_space=pl.ANY)
    return pl.pallas_call(
        kernel,
        out_shape=(
            jax.ShapeDtypeStruct((D, HID), bf16),
            jax.ShapeDtypeStruct((HID, D), bf16),
            jax.ShapeDtypeStruct((1, ROWS, D), bf16),
            jax.ShapeDtypeStruct((1, ROWS, D), bf16),
        ),
        in_specs=[vmem] * 5 + [hbm] * 4,
        out_specs=[hbm] * 2 + [vmem] * 2,
        scratch_shapes=[
            pltpu.VMEM((12, 8, PAD, D), bf16),
            pltpu.VMEM((2, D, HID), bf16),
            pltpu.VMEM((2, HID, D), bf16),
            pltpu.VMEM((4, 8 * PAD, HID), bf16),
            pltpu.VMEM((4, 8 * PAD, HID), bf16),
            pltpu.VMEM((4, 8, PAD, D), bf16),
            pltpu.VMEM((4, 8, PAD, D), bf16),
            pltpu.VMEM((4, PAD, D), bf16),
            pltpu.VMEM((4, PAD, D), f32),
            pltpu.VMEM((4, PAD, 128), f32),
            pltpu.VMEM((PAD, D), f32),
            pltpu.VMEM((2, PAD, D), bf16),
            pltpu.VMEM((2, 8 * PAD, HID), bf16),
            pltpu.VMEM((2, 8 * PAD, HID), bf16),
            pltpu.VMEM((D, HID), f32),
            pltpu.VMEM((HID, D), f32),
            pltpu.VMEM((D, HID), bf16),
            pltpu.VMEM((HID, D), bf16),
            dma((4,)), dma((2, NT)),
            dma((12, 9)), dma((12, 9)),
            dma((4, 8)), dma((4, 8)),
            dma((2,)), dma((2,)),
            dma((4,)), dma((4,)),
            dma((2,)), dma((2,)), dma((2,)), dma((2,)),
        ],
        compiler_params=pltpu.CompilerParams(
            collective_id=0, has_side_effects=True, vmem_limit_bytes=58 * 2**20
        ),
        cost_estimate=pl.CostEstimate(flops=11 * 10**9, bytes_accessed=13 * 10**6, transcendentals=10**6),
        name="relay_backward",
    )(*blocks)


def body(
    inputs_down, inputs_up, grads_down, grads_up, loss_grads,
    first_down, second_down, first_up, second_up, momentum_first, momentum_second,
):
    total_first, total_second, passed_down, passed_up = backward(
        inputs_down, inputs_up, grads_down, grads_up, loss_grads, first_down, second_down, first_up, second_up
    )
    new = []
    for weight, momentum, total in (
        (first_down, momentum_first, total_first), (second_down, momentum_second, total_second)
    ):
        moment = momentum_decay * momentum.astype(jnp.float32) + total[None].astype(jnp.float32)
        new.append(((weight.astype(jnp.float32) - learning_rate * moment).astype(jnp.bfloat16), moment.astype(jnp.bfloat16)))
    return (new[0][0], new[1][0], new[0][1], new[1][1], passed_down, passed_up)


def solution(mesh):
    placed = (
        P("section", None, "tensor", None),
        P("section", None, "tensor", None),
        P("section", "tensor", None),
        P("section", "tensor", None),
        P(None, "tensor", None),
        P("section", None, "tensor"),
        P("section", "tensor", None),
        P("section", None, "tensor"),
        P("section", "tensor", None),
        P("section", None, "tensor"),
        P("section", "tensor", None),
    )
    return jax.shard_map(
        body,
        mesh=mesh,
        in_specs=placed,
        out_specs=(
            P("section", None, "tensor"),
            P("section", "tensor", None),
            P("section", None, "tensor"),
            P("section", "tensor", None),
            P("section", "tensor", None),
            P("section", "tensor", None),
        ),
        check_vma=False,
    )
```

```python
import functools

import jax
import jax.numpy as jnp
from jax import lax
from jax.experimental import pallas as pl
from jax.experimental.pallas import tpu as pltpu
from jax.sharding import PartitionSpec as P

D = 2048
FF = 4096
ROWS = 30
PAD = 32
HID = 512
TILE = 256
MESH = pl.DeviceIdType.MESH

epsilon = 1e-05
learning_rate = 0.25
momentum_decay = 0.9
tanh_scale = 0.7978845608028654
cubic_term = 0.044715

N1U, C1U, N2U, C2U, N1D, C1D, N2D, C2D, N1M, C1M, N2M, C2M = range(12)
U1, U2, D1, D2 = range(4)
NT = D // TILE
HALF = PAD // 2
MODES = (1, 0, 0, 0, 0, 0, 1, 0, 0, 1, 1, 0)
SCHEDULE = (
    ("stage", N1U, 0), ("stage", C1U, 0), ("row", N1U), ("rest",), ("stage", C1D, 0), ("stage", N1U, 1),
    ("stage", C1U, 1), ("stage", N1D, 0), ("stage", N1U, 2), ("stage", C1D, 1), ("stage", C1U, 2), ("row", N2U),
    ("stage", N1D, 1), ("row", C1U), ("stage", N2D, 0), ("stage", C1D, 2), ("hidden", U1), ("stage", N1D, 2),
    ("stage", N2M, 0), ("mirror", U1), ("pair", U1), ("hidden", D1), ("cross", U1), ("stage", N1M, 0),
    ("pair", D1), ("finish", U1), ("stage", N2U, 0), ("cross", D1), ("relayed", 0), ("stage", C1M, 0),
    ("stage", C2U, 0), ("finish", D1), ("row", C2U), ("stage", C1M, 1), ("stage", N2M, 1), ("relayed", 1),
    ("stage", C2U, 1), ("stage", C2D, 0), ("stage", N2D, 1), ("stage", C2U, 2), ("stage", N2U, 1),
    ("stage", C2M, 0), ("stage", C1M, 2), ("stage", N2D, 2), ("stage", N2U, 2), ("stage", N1M, 1),
    ("stage", C2D, 1), ("add", 1), ("hidden", U2), ("partial", U2), ("mirror", U2), ("stage", C2D, 2),
    ("stage", N1M, 2), ("stage", N2M, 2), ("pair", U2), ("hidden", D2), ("add", 2), ("stage", C2M, 1),
    ("cross", U2), ("pair", D2), ("finish", U2), ("cross", D2), ("stage", C2M, 2), ("add", 3), ("finish", D2),
)


def gelu_with_slope(preact):
    tanh_input = tanh_scale * (preact + cubic_term * preact * preact * preact)
    tangent = jnp.tanh(tanh_input)
    values = 0.5 * preact * (1.0 + tangent)
    slopes = 0.5 * (1.0 + tangent) + 0.5 * preact * (1.0 - tangent * tangent) * tanh_scale * (
        1.0 + 3.0 * cubic_term * preact * preact
    )
    return (values, slopes)


def dot_nt(a, b):
    return lax.dot_general(a, b, (((1,), (1,)), ((), ())), preferred_element_type=jnp.float32)


def dot_tn(a, b):
    return lax.dot_general(a, b, (((0,), (0,)), ((), ())), preferred_element_type=jnp.float32)


def kernel(
    in_down, in_up, g_down, g_up, loss, w1d_h, w2d_h, w1u_h, w2u_h,
    t1_h, t2_h, pass_d, pass_u,
    G, W1, W2, A, GP, PB, RR, RH, ZB, NR, SC, CT, RL, MG, MA, ACC1, ACC2, T1, T2,
    load_sem, out_sem, ag_s, ag_r, rs_s, rs_r, rl_s, rl_r, row_s, row_r, mg_s, mg_r, ma_s, ma_r,
):
    s = lax.axis_index("section")
    t = lax.axis_index("tensor")
    x = lax.rem(t, 4)
    zh = t // 4
    zo = 1 - zh

    def xpeer(k):
        return (s, zh * 4 + lax.rem(x + k, 4))

    zpeer = (s, zo * 4 + x)
    mirror = (15 - s, t)
    up = (lax.rem(s + 1, 16), t)
    down = (lax.rem(s + 15, 16), t)

    barrier = pltpu.get_barrier_semaphore()
    for peer in (xpeer(1), xpeer(3), zpeer, mirror, up, down):
        pl.semaphore_signal(barrier, inc=1, device_id=peer, device_id_type=MESH)

    loads = []
    for i, (src, dst) in enumerate(
        ((w1u_h, W1.at[0]), (w2u_h, W2.at[0]), (w1d_h, W1.at[1]), (w2d_h, W2.at[1]))
    ):
        c = pltpu.make_async_copy(src.at[0], dst, load_sem.at[i])
        c.start()
        loads.append(c)

    def put_normed(ref, step, q, a):
        wide = ref[...].astype(jnp.float32)[:, step]
        centred = wide - jnp.mean(wide, axis=-1, keepdims=True)
        inv = lax.rsqrt(jnp.mean(centred * centred, axis=-1, keepdims=True) + epsilon)
        NR[q, ROWS:PAD] = jnp.zeros((PAD - ROWS, D), jnp.float32)
        NR[q, 0:ROWS] = centred * inv
        SC[q, ROWS:PAD] = jnp.zeros((PAD - ROWS, 128), jnp.float32)
        SC[q, 0:ROWS] = jnp.broadcast_to(inv, (ROWS, 128))
        G[a, t] = NR[q].astype(jnp.bfloat16)

    def put_rows(value, a):
        CT[ROWS:PAD] = jnp.zeros((PAD - ROWS, D), jnp.float32)
        CT[0:ROWS] = value.astype(jnp.float32)
        G[a, t] = CT[...].astype(jnp.bfloat16)

    def rcopy(src, dst, ss, rs, dev):
        return pltpu.make_async_remote_copy(
            src_ref=src, dst_ref=dst, send_sem=ss, recv_sem=rs, device_id=dev, device_id_type=MESH
        )

    pending = []

    def send(src, dst, ss, rs, dev):
        c = rcopy(src, dst, ss, rs, dev)
        c.start()
        pending.append(c)

    waited = set()

    def ag_ref(a, slot, half=None):
        return G.at[a, slot] if half is None else G.at[a, slot, pl.ds(half * HALF, HALF)]

    def ag_send(a, i, dev, slot, half=None):
        ref = ag_ref(a, slot, half)
        send(ref, ref, ag_s.at[a, i], ag_r.at[a, i], dev)

    def near(k):
        return zh * 4 + lax.rem(x + k, 4)

    def far(k):
        return zo * 4 + lax.rem(x + k, 4)

    def landing(a, i):
        first = MODES[a] == 0
        return (
            (far(0), None), (near(3), None), (near(1), None), (near(2), 0), (near(2), 1),
            (far(3), None), (far(1), None),
            (far(2), 0 if first else None), (far(2), 1),
        )[i]

    def ag_wait(a, *which):
        for i in which:
            if (a, i) not in waited:
                waited.add((a, i))
                ref = ag_ref(a, *landing(a, i))
                rcopy(ref, ref, ag_s.at[a, i], ag_r.at[a, i], zpeer).wait_recv()

    def ag_done(a):
        ag_wait(a, *range(9 if MODES[a] == 0 else 8))

    def row_wait(i):
        ref = G.at[N1M + i, t]
        rcopy(ref, ref, row_s.at[i], row_r.at[i], mirror).wait_recv()

    def stage(a, k):
        first = MODES[a] == 0
        if k == 0:
            if a >= N1M:
                row_wait(a - N1M)
            if first:
                ag_send(a, 0, zpeer, t)
            ag_send(a, 1, xpeer(1), t)
            ag_send(a, 2, xpeer(3), t)
            if not first:
                ag_send(a, 0, zpeer, t)
        elif k == 1:
            ag_wait(a, 1)
            ag_send(a, 3, xpeer(1), near(3), 0)
            if not first:
                ag_send(a, 5, zpeer, near(3))
            ag_wait(a, 2)
            ag_send(a, 4, xpeer(3), near(1), 1)
            if not first:
                ag_send(a, 6, zpeer, near(1))
            else:
                ag_wait(a, 0)
                ag_send(a, 5, xpeer(1), far(0))
                ag_send(a, 6, xpeer(3), far(0))
        elif first:
            ag_wait(a, 5)
            ag_send(a, 7, xpeer(1), far(3), 0)
            ag_wait(a, 6)
            ag_send(a, 8, xpeer(3), far(1), 1)
        else:
            ag_wait(a, 3, 4)
            ag_send(a, 7, zpeer, near(2))

    def row(a):
        send(G.at[a, t], G.at[N1M + a, t], row_s.at[a], row_r.at[a], mirror)

    def hidden(q, w, an, ac):
        @pl.loop(0, HID // TILE)
        def _(j):
            cols = pl.ds(pl.multiple_of(j * TILE, TILE), TILE)
            n = G[an].reshape(8 * PAD, D)
            pre = jnp.dot(n, W1[w, :, cols], preferred_element_type=jnp.float32) * D ** (-0.5)
            values, slopes = gelu_with_slope(pre)
            A[q, :, cols] = values.astype(jnp.bfloat16)
            c = G[ac].reshape(8 * PAD, D)
            ga = dot_nt(c, W2[w, cols, :]) * FF ** (-0.5)
            GP[q, :, cols] = (ga * slopes).astype(jnp.bfloat16)

    def partial(q, w):
        @pl.loop(0, NT)
        def _(j):
            cols = pl.ds(pl.multiple_of(j * TILE, TILE), TILE)
            part = dot_nt(GP[q], W1[w, cols, :]) * D ** (-0.5)
            PB[q, :, :, cols] = part.astype(jnp.bfloat16).reshape(8, PAD, TILE)

    def rs_send(q, i, src, dst, dev):
        send(src, dst, rs_s.at[q, i], rs_r.at[q, i], dev)

    def rs_start(q):
        for i, block in ((0, far(2)), (2, near(2))):
            rs_send(q, 5 + i, PB.at[q, block, pl.ds(0, HALF)], RH.at[q, i], xpeer(1))
            rs_send(q, 6 + i, PB.at[q, block, pl.ds(HALF, HALF)], RH.at[q, i + 1], xpeer(3))

    def rs_wait(q, i):
        ref = RR.at[q, i] if i < 5 else RH.at[q, i - 5]
        rcopy(ref, ref, rs_s.at[q, i], rs_r.at[q, i], zpeer).wait_recv()

    def rs_pair(q):
        for i, place in ((0, far), (2, near)):
            for k, half in ((1, 0), (3, 1)):
                rs_wait(q, 5 + i + half)
                rows = pl.ds(half * HALF, HALF)
                both = PB[q, place(k), rows].astype(jnp.float32) + RH[q, i + half].astype(jnp.float32)
                PB[q, place(k), rows] = both.astype(jnp.bfloat16)
                rs_send(q, 1 + i + half, PB.at[q, place(k)], RR.at[q, 1 + i + half], xpeer(k))

    def rs_mid(q):
        rs_wait(q, 1)
        rs_wait(q, 2)
        total = PB[q, far(0)].astype(jnp.float32) + RR[q, 1].astype(jnp.float32) + RR[q, 2].astype(jnp.float32)
        ZB[q] = total.astype(jnp.bfloat16)
        rs_send(q, 0, ZB.at[q], RR.at[q, 0], zpeer)

    def rs_end(q, ac):
        rs_wait(q, 3)
        rs_wait(q, 4)
        total = PB[q, t].astype(jnp.float32) + RR[q, 3].astype(jnp.float32) + RR[q, 4].astype(jnp.float32)
        rs_wait(q, 0)
        gn = total + RR[q, 0].astype(jnp.float32)
        normed = NR[q]
        first_mean = jnp.mean(gn, axis=-1, keepdims=True)
        second_mean = jnp.mean(gn * normed, axis=-1, keepdims=True)
        return G[ac, t].astype(jnp.float32) + SC[q, :, 0:1] * (gn - first_mean - normed * second_mean)

    def relay(q, ac, i, a, dev):
        RL[i] = rs_end(q, ac).astype(jnp.bfloat16)
        send(RL.at[i], G.at[a, t], rl_s.at[i], rl_r.at[i], dev)

    def relay_wait(i, a, edge, which):
        rcopy(RL.at[i], G.at[a, t], rl_s.at[i], rl_r.at[i], zpeer).wait_recv()

        @pl.when(s == edge)
        def _():
            put_rows(loss[...].astype(jnp.float32)[:, which], a)

    def mirror_hidden(q):
        send(GP.at[q], MG.at[q], mg_s.at[q], mg_r.at[q], mirror)
        send(A.at[q], MA.at[q], ma_s.at[q], ma_r.at[q], mirror)

    def mirror_wait(q):
        rcopy(GP.at[q], MG.at[q], mg_s.at[q], mg_r.at[q], mirror).wait_recv()
        rcopy(A.at[q], MA.at[q], ma_s.at[q], ma_r.at[q], mirror).wait_recv()

    def flat(a, cols):
        return G[a, :, :, cols].reshape(8 * PAD, TILE)

    def out_copies(j):
        cols = pl.ds(pl.multiple_of(j * TILE, TILE), TILE)
        return (
            pltpu.make_async_copy(T1.at[cols, :], t1_h.at[cols, :], out_sem.at[0, j]),
            pltpu.make_async_copy(T2.at[:, cols], t2_h.at[:, cols], out_sem.at[1, j]),
        )

    def add_terms(terms, first=False, last=False):
        @pl.loop(0, NT)
        def _(j):
            cols = pl.ds(pl.multiple_of(j * TILE, TILE), TILE)
            one = sum(dot_tn(flat(n, cols), gp[q]) for n, c, gp, ac, q in terms)
            two = sum(dot_tn(ac[q], flat(c, cols)) for n, c, gp, ac, q in terms)
            if not first:
                one = one + ACC1[cols, :]
                two = two + ACC2[:, cols]
            if last:
                T1[cols, :] = (one * D ** (-0.5)).astype(jnp.bfloat16)
                T2[:, cols] = (two * FF ** (-0.5)).astype(jnp.bfloat16)
                for c in out_copies(j):
                    c.start()
            else:
                ACC1[cols, :] = one
                ACC2[:, cols] = two

    sources = {U1: (0, N1U, C1U), U2: (0, N2U, C2U), D1: (1, N1D, C1D), D2: (1, N2D, C2D)}

    def branch(q):
        w, an, ac = sources[q]
        for i in (2 * w, 2 * w + 1):
            if i not in waited:
                waited.add(i)
                loads[i].wait()
        ag_done(an)
        ag_done(ac)
        hidden(q, w, an, ac)
        if q != U2:
            spread(q)

    def spread(q):
        partial(q, sources[q][0])
        rs_start(q)

    def finish(q):
        if q == U1:
            relay(q, C1U, 0, C2U, up)
        elif q == D1:
            relay(q, C1D, 1, C2D, down)
        else:
            CT[...] = rs_end(q, sources[q][2])
            (pass_u if q == U2 else pass_d)[0] = CT[0:ROWS].astype(jnp.bfloat16)

    def relayed(i):
        if i == 0:
            relay_wait(0, C2U, 0, 1)
        else:
            relay_wait(1, C2D, 15, 0)

    def rest():
        put_normed(in_down, 0, D1, N1D)
        put_rows(g_down[0], C1D)
        put_normed(in_up, 1, U2, N2U)
        put_normed(in_down, 1, D2, N2D)

    def add(part):
        if part == 1:
            add_terms([(N1D, C1D, GP, A, D1)], first=True)
        elif part == 2:
            ag_done(N1M)
            ag_done(C1M)
            mirror_wait(U1)
            add_terms([(N2D, C2D, GP, A, D2), (N1M, C1M, MG, MA, U1)])
        else:
            ag_done(N2M)
            ag_done(C2M)
            mirror_wait(U2)
            add_terms([(N2M, C2M, MG, MA, U2)], last=True)

    steps = dict(
        stage=stage, row=row, rest=rest, add=add, relayed=relayed, hidden=branch, mirror=mirror_hidden,
        partial=spread, pair=rs_pair, cross=rs_mid, finish=finish,
    )
    put_rows(g_up[0], C1U)
    put_normed(in_up, 0, U1, N1U)
    pl.semaphore_wait(barrier, 6)
    for step, *where in SCHEDULE:
        steps[step](*where)
    for c in pending:
        c.wait_send()

    @pl.loop(0, NT)
    def _(j):
        for c in out_copies(j):
            c.wait()


def backward(*blocks):
    bf16, f32 = jnp.bfloat16, jnp.float32
    dma = pltpu.SemaphoreType.DMA
    vmem = pl.BlockSpec(memory_space=pltpu.VMEM)
    hbm = pl.BlockSpec(memory_space=pl.ANY)
    return pl.pallas_call(
        kernel,
        out_shape=(
            jax.ShapeDtypeStruct((D, HID), bf16),
            jax.ShapeDtypeStruct((HID, D), bf16),
            jax.ShapeDtypeStruct((1, ROWS, D), bf16),
            jax.ShapeDtypeStruct((1, ROWS, D), bf16),
        ),
        in_specs=[vmem] * 5 + [hbm] * 4,
        out_specs=[hbm] * 2 + [vmem] * 2,
        scratch_shapes=[
            pltpu.VMEM((12, 8, PAD, D), bf16),
            pltpu.VMEM((2, D, HID), bf16),
            pltpu.VMEM((2, HID, D), bf16),
            pltpu.VMEM((4, 8 * PAD, HID), bf16),
            pltpu.VMEM((4, 8 * PAD, HID), bf16),
            pltpu.VMEM((4, 8, PAD, D), bf16),
            pltpu.VMEM((4, 5, PAD, D), bf16),
            pltpu.VMEM((4, 4, HALF, D), bf16),
            pltpu.VMEM((4, PAD, D), bf16),
            pltpu.VMEM((4, PAD, D), f32),
            pltpu.VMEM((4, PAD, 128), f32),
            pltpu.VMEM((PAD, D), f32),
            pltpu.VMEM((2, PAD, D), bf16),
            pltpu.VMEM((2, 8 * PAD, HID), bf16),
            pltpu.VMEM((2, 8 * PAD, HID), bf16),
            pltpu.VMEM((D, HID), f32),
            pltpu.VMEM((HID, D), f32),
            pltpu.VMEM((D, HID), bf16),
            pltpu.VMEM((HID, D), bf16),
            dma((4,)), dma((2, NT)),
            dma((12, 9)), dma((12, 9)),
            dma((4, 9)), dma((4, 9)),
            dma((2,)), dma((2,)),
            dma((4,)), dma((4,)),
            dma((2,)), dma((2,)), dma((2,)), dma((2,)),
        ],
        compiler_params=pltpu.CompilerParams(
            collective_id=0, has_side_effects=True, vmem_limit_bytes=58 * 2**20
        ),
        cost_estimate=pl.CostEstimate(flops=11 * 10**9, bytes_accessed=13 * 10**6, transcendentals=10**6),
        name="relay_backward",
    )(*blocks)


def body(
    inputs_down, inputs_up, grads_down, grads_up, loss_grads,
    first_down, second_down, first_up, second_up, momentum_first, momentum_second,
):
    total_first, total_second, passed_down, passed_up = backward(
        jnp.swapaxes(inputs_down[0], 0, 1), jnp.swapaxes(inputs_up[0], 0, 1), grads_down, grads_up,
        jnp.swapaxes(loss_grads, 0, 1), first_down, second_down, first_up, second_up,
    )
    new = []
    for weight, momentum, total in (
        (first_down, momentum_first, total_first), (second_down, momentum_second, total_second)
    ):
        moment = momentum_decay * momentum.astype(jnp.float32) + total[None].astype(jnp.float32)
        new.append(((weight.astype(jnp.float32) - learning_rate * moment).astype(jnp.bfloat16), moment.astype(jnp.bfloat16)))
    return (new[0][0], new[1][0], new[0][1], new[1][1], passed_down, passed_up)


def solution(mesh):
    placed = (
        P("section", None, "tensor", None),
        P("section", None, "tensor", None),
        P("section", "tensor", None),
        P("section", "tensor", None),
        P(None, "tensor", None),
        P("section", None, "tensor"),
        P("section", "tensor", None),
        P("section", None, "tensor"),
        P("section", "tensor", None),
        P("section", None, "tensor"),
        P("section", "tensor", None),
    )
    return jax.shard_map(
        body,
        mesh=mesh,
        in_specs=placed,
        out_specs=(
            P("section", None, "tensor"),
            P("section", "tensor", None),
            P("section", None, "tensor"),
            P("section", "tensor", None),
            P("section", "tensor", None),
            P("section", "tensor", None),
        ),
        check_vma=False,
    )
```

```python
import functools

import jax
import jax.numpy as jnp
from jax import lax
from jax.experimental import pallas as pl
from jax.experimental.pallas import tpu as pltpu
from jax.sharding import PartitionSpec as P

D = 2048
FF = 4096
ROWS = 30
PAD = 32
HID = 512
TILE = 256
MESH = pl.DeviceIdType.MESH

epsilon = 1e-05
learning_rate = 0.25
momentum_decay = 0.9
tanh_scale = 0.7978845608028654
cubic_term = 0.044715

N1U, C1U, N2U, C2U, N1D, C1D, N2D, C2D, N1M, C1M, N2M, C2M = range(12)
U1, U2, D1, D2 = range(4)
NT = D // TILE
HALF = PAD // 2
MODES = (1, 0, 1, 0, 0, 1, 0, 0, 0, 1, 1, 0)
SCHEDULE = (
    ("stage", C1U, 0), ("row", C1U), ("stage", N1U, 0), ("rest",), ("row", N1U), ("stage", N1D, 0),
    ("stage", N1U, 1), ("stage", C1U, 1), ("stage", N1U, 2), ("stage", C1D, 0), ("stage", C1U, 2),
    ("stage", N2D, 0), ("stage", C1D, 1), ("stage", N1D, 1), ("stage", C1M, 0), ("hidden", U1),
    ("stage", C1D, 2), ("stage", N1D, 2), ("pair", U1), ("stage", N1M, 0), ("stage", N2U, 0), ("cross", U1),
    ("row", N2U), ("stage", C1M, 1), ("hidden", D1), ("stage", N1M, 1), ("finish", U1), ("pair", D1),
    ("stage", N2U, 1), ("add", 1), ("relayed", 0), ("stage", C2U, 0), ("cross", D1), ("row", C2U),
    ("stage", N2M, 0), ("stage", N2D, 1), ("stage", C2U, 1), ("stage", N2U, 2), ("finish", D1),
    ("stage", C2M, 0), ("relayed", 1), ("stage", C2D, 0), ("mirror", U1), ("stage", C2U, 2), ("stage", C2M, 1),
    ("stage", C2D, 1), ("stage", N2D, 2), ("stage", C1M, 2), ("hidden", U2), ("partial", U2), ("mirror", U2),
    ("stage", C2D, 2), ("stage", N1M, 2), ("pair", U2), ("stage", N2M, 1), ("hidden", D2), ("stage", C2M, 2),
    ("add", 2), ("cross", U2), ("stage", N2M, 2), ("pair", D2), ("cross", D2), ("finish", U2), ("add", 3),
    ("finish", D2),
)


def gelu_with_slope(preact):
    tanh_input = tanh_scale * (preact + cubic_term * preact * preact * preact)
    tangent = jnp.tanh(tanh_input)
    values = 0.5 * preact * (1.0 + tangent)
    slopes = 0.5 * (1.0 + tangent) + 0.5 * preact * (1.0 - tangent * tangent) * tanh_scale * (
        1.0 + 3.0 * cubic_term * preact * preact
    )
    return (values, slopes)


def dot_nt(a, b):
    return lax.dot_general(a, b, (((1,), (1,)), ((), ())), preferred_element_type=jnp.float32)


def dot_tn(a, b):
    return lax.dot_general(a, b, (((0,), (0,)), ((), ())), preferred_element_type=jnp.float32)


def kernel(
    in_down, in_up, g_down, g_up, loss, w1d_h, w2d_h, w1u_h, w2u_h,
    t1_h, t2_h, pass_d, pass_u,
    G, W1, W2, A, GP, PB, RR, RH, ZB, NR, SC, CT, RL, MG, MA, ACC1, ACC2, T1, T2,
    load_sem, out_sem, ag_s, ag_r, rs_s, rs_r, rl_s, rl_r, row_s, row_r, mg_s, mg_r, ma_s, ma_r,
):
    s = lax.axis_index("section")
    t = lax.axis_index("tensor")
    x = lax.rem(t, 4)
    zh = t // 4
    zo = 1 - zh

    def xpeer(k):
        return (s, zh * 4 + lax.rem(x + k, 4))

    zpeer = (s, zo * 4 + x)
    mirror = (15 - s, t)
    up = (lax.rem(s + 1, 16), t)
    down = (lax.rem(s + 15, 16), t)

    barrier = pltpu.get_barrier_semaphore()
    for peer in (xpeer(1), xpeer(3), zpeer, mirror, up, down):
        pl.semaphore_signal(barrier, inc=1, device_id=peer, device_id_type=MESH)

    loads = []
    for i, (src, dst) in enumerate(
        ((w1u_h, W1.at[0]), (w2u_h, W2.at[0]), (w1d_h, W1.at[1]), (w2d_h, W2.at[1]))
    ):
        c = pltpu.make_async_copy(src.at[0], dst, load_sem.at[i])
        c.start()
        loads.append(c)

    def put_normed(ref, step, q, a):
        wide = ref[...].astype(jnp.float32)[:, step]
        centred = wide - jnp.mean(wide, axis=-1, keepdims=True)
        inv = lax.rsqrt(jnp.mean(centred * centred, axis=-1, keepdims=True) + epsilon)
        NR[q, ROWS:PAD] = jnp.zeros((PAD - ROWS, D), jnp.float32)
        NR[q, 0:ROWS] = centred * inv
        SC[q, ROWS:PAD] = jnp.zeros((PAD - ROWS, 128), jnp.float32)
        SC[q, 0:ROWS] = jnp.broadcast_to(inv, (ROWS, 128))
        G[a, t] = NR[q].astype(jnp.bfloat16)

    def put_rows(value, a):
        CT[ROWS:PAD] = jnp.zeros((PAD - ROWS, D), jnp.float32)
        CT[0:ROWS] = value.astype(jnp.float32)
        G[a, t] = CT[...].astype(jnp.bfloat16)

    def rcopy(src, dst, ss, rs, dev):
        return pltpu.make_async_remote_copy(
            src_ref=src, dst_ref=dst, send_sem=ss, recv_sem=rs, device_id=dev, device_id_type=MESH
        )

    pending = []

    def send(src, dst, ss, rs, dev):
        c = rcopy(src, dst, ss, rs, dev)
        c.start()
        pending.append(c)

    waited = set()

    def ag_ref(a, slot, half=None):
        return G.at[a, slot] if half is None else G.at[a, slot, pl.ds(half * HALF, HALF)]

    def ag_send(a, i, dev, slot, half=None):
        ref = ag_ref(a, slot, half)
        send(ref, ref, ag_s.at[a, i], ag_r.at[a, i], dev)

    def near(k):
        return zh * 4 + lax.rem(x + k, 4)

    def far(k):
        return zo * 4 + lax.rem(x + k, 4)

    def landing(a, i):
        first = MODES[a] == 0
        return (
            (far(0), None), (near(3), None), (near(1), None), (near(2), 0), (near(2), 1),
            (far(3), None), (far(1), None),
            (far(2), 0 if first else None), (far(2), 1),
        )[i]

    def ag_wait(a, *which):
        for i in which:
            if (a, i) not in waited:
                waited.add((a, i))
                ref = ag_ref(a, *landing(a, i))
                rcopy(ref, ref, ag_s.at[a, i], ag_r.at[a, i], zpeer).wait_recv()

    def ag_done(a):
        ag_wait(a, *range(9 if MODES[a] == 0 else 8))

    def row_wait(i):
        ref = G.at[N1M + i, t]
        rcopy(ref, ref, row_s.at[i], row_r.at[i], mirror).wait_recv()

    def stage(a, k):
        first = MODES[a] == 0
        if k == 0:
            if a >= N1M:
                row_wait(a - N1M)
            if first:
                ag_send(a, 0, zpeer, t)
            ag_send(a, 1, xpeer(1), t)
            ag_send(a, 2, xpeer(3), t)
            if not first:
                ag_send(a, 0, zpeer, t)
        elif k == 1:
            ag_wait(a, 1)
            ag_send(a, 3, xpeer(1), near(3), 0)
            if not first:
                ag_send(a, 5, zpeer, near(3))
            ag_wait(a, 2)
            ag_send(a, 4, xpeer(3), near(1), 1)
            if not first:
                ag_send(a, 6, zpeer, near(1))
            else:
                ag_wait(a, 0)
                ag_send(a, 5, xpeer(1), far(0))
                ag_send(a, 6, xpeer(3), far(0))
        elif first:
            ag_wait(a, 5)
            ag_send(a, 7, xpeer(1), far(3), 0)
            ag_wait(a, 6)
            ag_send(a, 8, xpeer(3), far(1), 1)
        else:
            ag_wait(a, 3, 4)
            ag_send(a, 7, zpeer, near(2))

    def row(a):
        send(G.at[a, t], G.at[N1M + a, t], row_s.at[a], row_r.at[a], mirror)

    def hidden(q, w, an, ac):
        @pl.loop(0, HID // TILE)
        def _(j):
            cols = pl.ds(pl.multiple_of(j * TILE, TILE), TILE)
            n = G[an].reshape(8 * PAD, D)
            pre = jnp.dot(n, W1[w, :, cols], preferred_element_type=jnp.float32) * D ** (-0.5)
            values, slopes = gelu_with_slope(pre)
            A[q, :, cols] = values.astype(jnp.bfloat16)
            c = G[ac].reshape(8 * PAD, D)
            ga = dot_nt(c, W2[w, cols, :]) * FF ** (-0.5)
            GP[q, :, cols] = (ga * slopes).astype(jnp.bfloat16)

    def partial(q, w):
        @pl.loop(0, NT)
        def _(j):
            cols = pl.ds(pl.multiple_of(j * TILE, TILE), TILE)
            part = dot_nt(GP[q], W1[w, cols, :]) * D ** (-0.5)
            PB[q, :, :, cols] = part.astype(jnp.bfloat16).reshape(8, PAD, TILE)

    def rs_send(q, i, src, dst, dev):
        send(src, dst, rs_s.at[q, i], rs_r.at[q, i], dev)

    def rs_start(q):
        for i, block in ((0, far(2)), (2, near(2))):
            rs_send(q, 5 + i, PB.at[q, block, pl.ds(0, HALF)], RH.at[q, i], xpeer(1))
            rs_send(q, 6 + i, PB.at[q, block, pl.ds(HALF, HALF)], RH.at[q, i + 1], xpeer(3))

    def rs_wait(q, i):
        ref = RR.at[q, i] if i < 5 else RH.at[q, i - 5]
        rcopy(ref, ref, rs_s.at[q, i], rs_r.at[q, i], zpeer).wait_recv()

    def rs_pair(q):
        for i, place in ((0, far), (2, near)):
            for k, half in ((1, 0), (3, 1)):
                rs_wait(q, 5 + i + half)
                rows = pl.ds(half * HALF, HALF)
                both = PB[q, place(k), rows].astype(jnp.float32) + RH[q, i + half].astype(jnp.float32)
                PB[q, place(k), rows] = both.astype(jnp.bfloat16)
                rs_send(q, 1 + i + half, PB.at[q, place(k)], RR.at[q, 1 + i + half], xpeer(k))

    def rs_mid(q):
        rs_wait(q, 1)
        rs_wait(q, 2)
        total = PB[q, far(0)].astype(jnp.float32) + RR[q, 1].astype(jnp.float32) + RR[q, 2].astype(jnp.float32)
        ZB[q] = total.astype(jnp.bfloat16)
        rs_send(q, 0, ZB.at[q], RR.at[q, 0], zpeer)

    def rs_end(q, ac):
        rs_wait(q, 3)
        rs_wait(q, 4)
        total = PB[q, t].astype(jnp.float32) + RR[q, 3].astype(jnp.float32) + RR[q, 4].astype(jnp.float32)
        rs_wait(q, 0)
        gn = total + RR[q, 0].astype(jnp.float32)
        normed = NR[q]
        first_mean = jnp.mean(gn, axis=-1, keepdims=True)
        second_mean = jnp.mean(gn * normed, axis=-1, keepdims=True)
        return G[ac, t].astype(jnp.float32) + SC[q, :, 0:1] * (gn - first_mean - normed * second_mean)

    def relay(q, ac, i, a, dev):
        RL[i] = rs_end(q, ac).astype(jnp.bfloat16)
        send(RL.at[i], G.at[a, t], rl_s.at[i], rl_r.at[i], dev)

    def relay_wait(i, a, edge, which):
        rcopy(RL.at[i], G.at[a, t], rl_s.at[i], rl_r.at[i], zpeer).wait_recv()

        @pl.when(s == edge)
        def _():
            put_rows(loss[...].astype(jnp.float32)[:, which], a)

    def mirror_hidden(q):
        send(GP.at[q], MG.at[q], mg_s.at[q], mg_r.at[q], mirror)
        send(A.at[q], MA.at[q], ma_s.at[q], ma_r.at[q], mirror)

    def mirror_wait(q):
        rcopy(GP.at[q], MG.at[q], mg_s.at[q], mg_r.at[q], mirror).wait_recv()
        rcopy(A.at[q], MA.at[q], ma_s.at[q], ma_r.at[q], mirror).wait_recv()

    def flat(a, cols):
        return G[a, :, :, cols].reshape(8 * PAD, TILE)

    def out_copies(j):
        cols = pl.ds(pl.multiple_of(j * TILE, TILE), TILE)
        return (
            pltpu.make_async_copy(T1.at[cols, :], t1_h.at[cols, :], out_sem.at[0, j]),
            pltpu.make_async_copy(T2.at[:, cols], t2_h.at[:, cols], out_sem.at[1, j]),
        )

    def add_terms(terms, first=False, last=False):
        @pl.loop(0, NT)
        def _(j):
            cols = pl.ds(pl.multiple_of(j * TILE, TILE), TILE)
            one = sum(dot_tn(flat(n, cols), gp[q]) for n, c, gp, ac, q in terms)
            two = sum(dot_tn(ac[q], flat(c, cols)) for n, c, gp, ac, q in terms)
            if not first:
                one = one + ACC1[cols, :]
                two = two + ACC2[:, cols]
            if last:
                T1[cols, :] = (one * D ** (-0.5)).astype(jnp.bfloat16)
                T2[:, cols] = (two * FF ** (-0.5)).astype(jnp.bfloat16)
                for c in out_copies(j):
                    c.start()
            else:
                ACC1[cols, :] = one
                ACC2[:, cols] = two

    sources = {U1: (0, N1U, C1U), U2: (0, N2U, C2U), D1: (1, N1D, C1D), D2: (1, N2D, C2D)}

    def branch(q):
        w, an, ac = sources[q]
        for i in (2 * w, 2 * w + 1):
            if i not in waited:
                waited.add(i)
                loads[i].wait()
        ag_done(an)
        ag_done(ac)
        hidden(q, w, an, ac)
        if q != U2:
            spread(q)

    def spread(q):
        partial(q, sources[q][0])
        rs_start(q)

    def finish(q):
        if q == U1:
            relay(q, C1U, 0, C2U, up)
        elif q == D1:
            relay(q, C1D, 1, C2D, down)
        else:
            CT[...] = rs_end(q, sources[q][2])
            (pass_u if q == U2 else pass_d)[0] = CT[0:ROWS].astype(jnp.bfloat16)

    def relayed(i):
        if i == 0:
            relay_wait(0, C2U, 0, 1)
        else:
            relay_wait(1, C2D, 15, 0)

    def rest():
        put_normed(in_down, 0, D1, N1D)
        put_rows(g_down[0], C1D)
        put_normed(in_up, 1, U2, N2U)
        put_normed(in_down, 1, D2, N2D)

    def add(part):
        if part == 1:
            add_terms([(N1D, C1D, GP, A, D1)], first=True)
        elif part == 2:
            ag_done(N1M)
            ag_done(C1M)
            mirror_wait(U1)
            add_terms([(N2D, C2D, GP, A, D2), (N1M, C1M, MG, MA, U1)])
        else:
            ag_done(N2M)
            ag_done(C2M)
            mirror_wait(U2)
            add_terms([(N2M, C2M, MG, MA, U2)], last=True)

    steps = dict(
        stage=stage, row=row, rest=rest, add=add, relayed=relayed, hidden=branch, mirror=mirror_hidden,
        partial=spread, pair=rs_pair, cross=rs_mid, finish=finish,
    )
    put_rows(g_up[0], C1U)
    put_normed(in_up, 0, U1, N1U)
    pl.semaphore_wait(barrier, 6)
    for step, *where in SCHEDULE:
        steps[step](*where)
    for c in pending:
        c.wait_send()

    @pl.loop(0, NT)
    def _(j):
        for c in out_copies(j):
            c.wait()


def backward(*blocks):
    bf16, f32 = jnp.bfloat16, jnp.float32
    dma = pltpu.SemaphoreType.DMA
    vmem = pl.BlockSpec(memory_space=pltpu.VMEM)
    hbm = pl.BlockSpec(memory_space=pl.ANY)
    return pl.pallas_call(
        kernel,
        out_shape=(
            jax.ShapeDtypeStruct((D, HID), bf16),
            jax.ShapeDtypeStruct((HID, D), bf16),
            jax.ShapeDtypeStruct((1, ROWS, D), bf16),
            jax.ShapeDtypeStruct((1, ROWS, D), bf16),
        ),
        in_specs=[vmem] * 5 + [hbm] * 4,
        out_specs=[hbm] * 2 + [vmem] * 2,
        scratch_shapes=[
            pltpu.VMEM((12, 8, PAD, D), bf16),
            pltpu.VMEM((2, D, HID), bf16),
            pltpu.VMEM((2, HID, D), bf16),
            pltpu.VMEM((4, 8 * PAD, HID), bf16),
            pltpu.VMEM((4, 8 * PAD, HID), bf16),
            pltpu.VMEM((4, 8, PAD, D), bf16),
            pltpu.VMEM((4, 5, PAD, D), bf16),
            pltpu.VMEM((4, 4, HALF, D), bf16),
            pltpu.VMEM((4, PAD, D), bf16),
            pltpu.VMEM((4, PAD, D), f32),
            pltpu.VMEM((4, PAD, 128), f32),
            pltpu.VMEM((PAD, D), f32),
            pltpu.VMEM((2, PAD, D), bf16),
            pltpu.VMEM((2, 8 * PAD, HID), bf16),
            pltpu.VMEM((2, 8 * PAD, HID), bf16),
            pltpu.VMEM((D, HID), f32),
            pltpu.VMEM((HID, D), f32),
            pltpu.VMEM((D, HID), bf16),
            pltpu.VMEM((HID, D), bf16),
            dma((4,)), dma((2, NT)),
            dma((12, 9)), dma((12, 9)),
            dma((4, 9)), dma((4, 9)),
            dma((2,)), dma((2,)),
            dma((4,)), dma((4,)),
            dma((2,)), dma((2,)), dma((2,)), dma((2,)),
        ],
        compiler_params=pltpu.CompilerParams(
            collective_id=0, has_side_effects=True, vmem_limit_bytes=58 * 2**20
        ),
        cost_estimate=pl.CostEstimate(flops=11 * 10**9, bytes_accessed=13 * 10**6, transcendentals=10**6),
        name="relay_backward",
    )(*blocks)


def body(
    inputs_down, inputs_up, grads_down, grads_up, loss_grads,
    first_down, second_down, first_up, second_up, momentum_first, momentum_second,
):
    total_first, total_second, passed_down, passed_up = backward(
        jnp.swapaxes(inputs_down[0], 0, 1), jnp.swapaxes(inputs_up[0], 0, 1), grads_down, grads_up,
        jnp.swapaxes(loss_grads, 0, 1), first_down, second_down, first_up, second_up,
    )
    new = []
    for weight, momentum, total in (
        (first_down, momentum_first, total_first), (second_down, momentum_second, total_second)
    ):
        moment = momentum_decay * momentum.astype(jnp.float32) + total[None].astype(jnp.float32)
        new.append(((weight.astype(jnp.float32) - learning_rate * moment).astype(jnp.bfloat16), moment.astype(jnp.bfloat16)))
    return (new[0][0], new[1][0], new[0][1], new[1][1], passed_down, passed_up)


def solution(mesh):
    placed = (
        P("section", None, "tensor", None),
        P("section", None, "tensor", None),
        P("section", "tensor", None),
        P("section", "tensor", None),
        P(None, "tensor", None),
        P("section", None, "tensor"),
        P("section", "tensor", None),
        P("section", None, "tensor"),
        P("section", "tensor", None),
        P("section", None, "tensor"),
        P("section", "tensor", None),
    )
    return jax.shard_map(
        body,
        mesh=mesh,
        in_specs=placed,
        out_specs=(
            P("section", None, "tensor"),
            P("section", "tensor", None),
            P("section", None, "tensor"),
            P("section", "tensor", None),
            P("section", "tensor", None),
            P("section", "tensor", None),
        ),
        check_vma=False,
    )
```

```python
import functools

import jax
import jax.numpy as jnp
from jax import lax
from jax.experimental import pallas as pl
from jax.experimental.pallas import tpu as pltpu
from jax.sharding import PartitionSpec as P

D = 2048
FF = 4096
ROWS = 30
PAD = 32
HID = 512
TILE = 256
MESH = pl.DeviceIdType.MESH

epsilon = 1e-05
learning_rate = 0.25
momentum_decay = 0.9
tanh_scale = 0.7978845608028654
cubic_term = 0.044715

N1U, C1U, N2U, C2U, N1D, C1D, N2D, C2D, N1M, C1M, N2M, C2M = range(12)
U1, U2, D1, D2 = range(4)
NT = D // TILE
HALF = PAD // 2
MODES = (1, 0, 0, 0, 0, 1, 0, 0, 0, 1, 1, 0)
SCHEDULE = (
    ("stage", C1U, 0), ("row", C1U), ("stage", N1U, 0), ("rest",), ("row", N1U), ("stage", N1D, 0),
    ("stage", N1U, 1), ("stage", C1U, 1), ("stage", N1U, 2), ("stage", C1D, 0), ("stage", C1U, 2),
    ("stage", N2D, 0), ("stage", C1D, 1), ("stage", N1D, 1), ("stage", C1M, 0), ("hidden", U1),
    ("stage", C1D, 2), ("stage", N1D, 2), ("pair", U1), ("stage", N1M, 0), ("stage", N2U, 0), ("cross", U1),
    ("row", N2U), ("stage", C1M, 1), ("hidden", D1), ("stage", N1M, 1), ("finish", U1), ("pair", D1),
    ("stage", N2U, 1), ("add", 1), ("relayed", 0), ("stage", C2U, 0), ("cross", D1), ("row", C2U),
    ("stage", N2M, 0), ("stage", N2D, 1), ("stage", C2U, 1), ("stage", N2U, 2), ("finish", D1),
    ("stage", C2M, 0), ("relayed", 1), ("stage", C2D, 0), ("mirror", U1), ("stage", C2U, 2), ("stage", C2M, 1),
    ("stage", C2D, 1), ("stage", N2D, 2), ("stage", C1M, 2), ("hidden", U2), ("partial", U2), ("mirror", U2),
    ("stage", C2D, 2), ("stage", N1M, 2), ("pair", U2), ("stage", N2M, 1), ("hidden", D2), ("stage", C2M, 2),
    ("add", 2), ("cross", U2), ("stage", N2M, 2), ("pair", D2), ("cross", D2), ("finish", U2), ("add", 3),
    ("finish", D2),
)


def gelu_with_slope(preact):
    tanh_input = tanh_scale * (preact + cubic_term * preact * preact * preact)
    tangent = jnp.tanh(tanh_input)
    values = 0.5 * preact * (1.0 + tangent)
    slopes = 0.5 * (1.0 + tangent) + 0.5 * preact * (1.0 - tangent * tangent) * tanh_scale * (
        1.0 + 3.0 * cubic_term * preact * preact
    )
    return (values, slopes)


def dot_nt(a, b):
    return lax.dot_general(a, b, (((1,), (1,)), ((), ())), preferred_element_type=jnp.float32)


def dot_tn(a, b):
    return lax.dot_general(a, b, (((0,), (0,)), ((), ())), preferred_element_type=jnp.float32)


def kernel(
    in_down, in_up, g_down, g_up, loss, w1d_h, w2d_h, w1u_h, w2u_h,
    t1_h, t2_h, pass_d, pass_u,
    G, W1, W2, A, GP, PB, RR, RH, ZB, NR, SC, CT, RL, MG, MA, ACC1, ACC2, T1, T2,
    load_sem, out_sem, ag_s, ag_r, rs_s, rs_r, rl_s, rl_r, row_s, row_r, mg_s, mg_r, ma_s, ma_r,
):
    s = lax.axis_index("section")
    t = lax.axis_index("tensor")
    x = lax.rem(t, 4)
    zh = t // 4
    zo = 1 - zh

    def xpeer(k):
        return (s, zh * 4 + lax.rem(x + k, 4))

    zpeer = (s, zo * 4 + x)
    mirror = (15 - s, t)
    up = (lax.rem(s + 1, 16), t)
    down = (lax.rem(s + 15, 16), t)

    barrier = pltpu.get_barrier_semaphore()
    for peer in (xpeer(1), xpeer(3), zpeer, mirror, up, down):
        pl.semaphore_signal(barrier, inc=1, device_id=peer, device_id_type=MESH)

    loads = []
    for i, (src, dst) in enumerate(
        ((w1u_h, W1.at[0]), (w2u_h, W2.at[0]), (w1d_h, W1.at[1]), (w2d_h, W2.at[1]))
    ):
        c = pltpu.make_async_copy(src.at[0], dst, load_sem.at[i])
        c.start()
        loads.append(c)

    def put_normed(ref, step, q, a):
        wide = ref[...].astype(jnp.float32)[:, step]
        centred = wide - jnp.mean(wide, axis=-1, keepdims=True)
        inv = lax.rsqrt(jnp.mean(centred * centred, axis=-1, keepdims=True) + epsilon)
        NR[q, ROWS:PAD] = jnp.zeros((PAD - ROWS, D), jnp.float32)
        NR[q, 0:ROWS] = centred * inv
        SC[q, ROWS:PAD] = jnp.zeros((PAD - ROWS, 128), jnp.float32)
        SC[q, 0:ROWS] = jnp.broadcast_to(inv, (ROWS, 128))
        G[a, t] = NR[q].astype(jnp.bfloat16)

    def put_rows(value, a):
        CT[ROWS:PAD] = jnp.zeros((PAD - ROWS, D), jnp.float32)
        CT[0:ROWS] = value.astype(jnp.float32)
        G[a, t] = CT[...].astype(jnp.bfloat16)

    def rcopy(src, dst, ss, rs, dev):
        return pltpu.make_async_remote_copy(
            src_ref=src, dst_ref=dst, send_sem=ss, recv_sem=rs, device_id=dev, device_id_type=MESH
        )

    pending = []

    def send(src, dst, ss, rs, dev):
        c = rcopy(src, dst, ss, rs, dev)
        c.start()
        pending.append(c)

    waited = set()

    def ag_ref(a, slot, half=None):
        return G.at[a, slot] if half is None else G.at[a, slot, pl.ds(half * HALF, HALF)]

    def ag_send(a, i, dev, slot, half=None):
        ref = ag_ref(a, slot, half)
        send(ref, ref, ag_s.at[a, i], ag_r.at[a, i], dev)

    def near(k):
        return zh * 4 + lax.rem(x + k, 4)

    def far(k):
        return zo * 4 + lax.rem(x + k, 4)

    def landing(a, i):
        first = MODES[a] == 0
        return (
            (far(0), None), (near(3), None), (near(1), None), (near(2), 0), (near(2), 1),
            (far(3), None), (far(1), None),
            (far(2), 0 if first else None), (far(2), 1),
        )[i]

    def ag_wait(a, *which):
        for i in which:
            if (a, i) not in waited:
                waited.add((a, i))
                ref = ag_ref(a, *landing(a, i))
                rcopy(ref, ref, ag_s.at[a, i], ag_r.at[a, i], zpeer).wait_recv()

    def ag_done(a):
        ag_wait(a, *range(9 if MODES[a] == 0 else 8))

    def row_wait(i):
        ref = G.at[N1M + i, t]
        rcopy(ref, ref, row_s.at[i], row_r.at[i], mirror).wait_recv()

    def stage(a, k):
        first = MODES[a] == 0
        if k == 0:
            if a >= N1M:
                row_wait(a - N1M)
            if first:
                ag_send(a, 0, zpeer, t)
            ag_send(a, 1, xpeer(1), t)
            ag_send(a, 2, xpeer(3), t)
            if not first:
                ag_send(a, 0, zpeer, t)
        elif k == 1:
            ag_wait(a, 1)
            ag_send(a, 3, xpeer(1), near(3), 0)
            if not first:
                ag_send(a, 5, zpeer, near(3))
            ag_wait(a, 2)
            ag_send(a, 4, xpeer(3), near(1), 1)
            if not first:
                ag_send(a, 6, zpeer, near(1))
            else:
                ag_wait(a, 0)
                ag_send(a, 5, xpeer(1), far(0))
                ag_send(a, 6, xpeer(3), far(0))
        elif first:
            ag_wait(a, 5)
            ag_send(a, 7, xpeer(1), far(3), 0)
            ag_wait(a, 6)
            ag_send(a, 8, xpeer(3), far(1), 1)
        else:
            ag_wait(a, 3, 4)
            ag_send(a, 7, zpeer, near(2))

    def row(a):
        send(G.at[a, t], G.at[N1M + a, t], row_s.at[a], row_r.at[a], mirror)

    def hidden(q, w, an, ac):
        @pl.loop(0, HID // TILE)
        def _(j):
            cols = pl.ds(pl.multiple_of(j * TILE, TILE), TILE)
            n = G[an].reshape(8 * PAD, D)
            pre = jnp.dot(n, W1[w, :, cols], preferred_element_type=jnp.float32) * D ** (-0.5)
            values, slopes = gelu_with_slope(pre)
            A[q, :, cols] = values.astype(jnp.bfloat16)
            c = G[ac].reshape(8 * PAD, D)
            ga = dot_nt(c, W2[w, cols, :]) * FF ** (-0.5)
            GP[q, :, cols] = (ga * slopes).astype(jnp.bfloat16)

    def partial(q, w):
        @pl.loop(0, NT)
        def _(j):
            cols = pl.ds(pl.multiple_of(j * TILE, TILE), TILE)
            part = dot_nt(GP[q], W1[w, cols, :]) * D ** (-0.5)
            PB[q, :, :, cols] = part.astype(jnp.bfloat16).reshape(8, PAD, TILE)

    def rs_send(q, i, src, dst, dev):
        send(src, dst, rs_s.at[q, i], rs_r.at[q, i], dev)

    def rs_start(q):
        for i, block in ((0, far(2)), (2, near(2))):
            rs_send(q, 5 + i, PB.at[q, block, pl.ds(0, HALF)], RH.at[q, i], xpeer(1))
            rs_send(q, 6 + i, PB.at[q, block, pl.ds(HALF, HALF)], RH.at[q, i + 1], xpeer(3))

    def rs_wait(q, i):
        ref = RR.at[q, i] if i < 5 else RH.at[q, i - 5]
        rcopy(ref, ref, rs_s.at[q, i], rs_r.at[q, i], zpeer).wait_recv()

    def rs_pair(q):
        for i, place in ((0, far), (2, near)):
            for k, half in ((1, 0), (3, 1)):
                rs_wait(q, 5 + i + half)
                rows = pl.ds(half * HALF, HALF)
                both = PB[q, place(k), rows].astype(jnp.float32) + RH[q, i + half].astype(jnp.float32)
                PB[q, place(k), rows] = both.astype(jnp.bfloat16)
                rs_send(q, 1 + i + half, PB.at[q, place(k)], RR.at[q, 1 + i + half], xpeer(k))

    def rs_mid(q):
        rs_wait(q, 1)
        rs_wait(q, 2)
        total = PB[q, far(0)].astype(jnp.float32) + RR[q, 1].astype(jnp.float32) + RR[q, 2].astype(jnp.float32)
        ZB[q] = total.astype(jnp.bfloat16)
        rs_send(q, 0, ZB.at[q], RR.at[q, 0], zpeer)

    def rs_end(q, ac):
        rs_wait(q, 3)
        rs_wait(q, 4)
        total = PB[q, t].astype(jnp.float32) + RR[q, 3].astype(jnp.float32) + RR[q, 4].astype(jnp.float32)
        rs_wait(q, 0)
        gn = total + RR[q, 0].astype(jnp.float32)
        normed = NR[q]
        first_mean = jnp.mean(gn, axis=-1, keepdims=True)
        second_mean = jnp.mean(gn * normed, axis=-1, keepdims=True)
        return G[ac, t].astype(jnp.float32) + SC[q, :, 0:1] * (gn - first_mean - normed * second_mean)

    def relay(q, ac, i, a, dev):
        RL[i] = rs_end(q, ac).astype(jnp.bfloat16)
        send(RL.at[i], G.at[a, t], rl_s.at[i], rl_r.at[i], dev)

    def relay_wait(i, a, edge, which):
        rcopy(RL.at[i], G.at[a, t], rl_s.at[i], rl_r.at[i], zpeer).wait_recv()

        @pl.when(s == edge)
        def _():
            put_rows(loss[...].astype(jnp.float32)[:, which], a)

    def mirror_hidden(q):
        send(GP.at[q], MG.at[q], mg_s.at[q], mg_r.at[q], mirror)
        send(A.at[q], MA.at[q], ma_s.at[q], ma_r.at[q], mirror)

    def mirror_wait(q):
        rcopy(GP.at[q], MG.at[q], mg_s.at[q], mg_r.at[q], mirror).wait_recv()
        rcopy(A.at[q], MA.at[q], ma_s.at[q], ma_r.at[q], mirror).wait_recv()

    def flat(a, cols):
        return G[a, :, :, cols].reshape(8 * PAD, TILE)

    def out_copies(j):
        cols = pl.ds(pl.multiple_of(j * TILE, TILE), TILE)
        return (
            pltpu.make_async_copy(T1.at[cols, :], t1_h.at[cols, :], out_sem.at[0, j]),
            pltpu.make_async_copy(T2.at[:, cols], t2_h.at[:, cols], out_sem.at[1, j]),
        )

    def add_terms(terms, first=False, last=False):
        @pl.loop(0, NT)
        def _(j):
            cols = pl.ds(pl.multiple_of(j * TILE, TILE), TILE)
            one = sum(dot_tn(flat(n, cols), gp[q]) for n, c, gp, ac, q in terms)
            two = sum(dot_tn(ac[q], flat(c, cols)) for n, c, gp, ac, q in terms)
            if not first:
                one = one + ACC1[cols, :]
                two = two + ACC2[:, cols]
            if last:
                T1[cols, :] = (one * D ** (-0.5)).astype(jnp.bfloat16)
                T2[:, cols] = (two * FF ** (-0.5)).astype(jnp.bfloat16)
                for c in out_copies(j):
                    c.start()
            else:
                ACC1[cols, :] = one
                ACC2[:, cols] = two

    sources = {U1: (0, N1U, C1U), U2: (0, N2U, C2U), D1: (1, N1D, C1D), D2: (1, N2D, C2D)}

    def branch(q):
        w, an, ac = sources[q]
        for i in (2 * w, 2 * w + 1):
            if i not in waited:
                waited.add(i)
                loads[i].wait()
        ag_done(an)
        ag_done(ac)
        hidden(q, w, an, ac)
        if q != U2:
            spread(q)

    def spread(q):
        partial(q, sources[q][0])
        rs_start(q)

    def finish(q):
        if q == U1:
            relay(q, C1U, 0, C2U, up)
        elif q == D1:
            relay(q, C1D, 1, C2D, down)
        else:
            CT[...] = rs_end(q, sources[q][2])
            (pass_u if q == U2 else pass_d)[0] = CT[0:ROWS].astype(jnp.bfloat16)

    def relayed(i):
        if i == 0:
            relay_wait(0, C2U, 0, 1)
        else:
            relay_wait(1, C2D, 15, 0)

    def rest():
        put_normed(in_down, 0, D1, N1D)
        put_rows(g_down[0], C1D)
        put_normed(in_up, 1, U2, N2U)
        put_normed(in_down, 1, D2, N2D)

    def add(part):
        if part == 1:
            add_terms([(N1D, C1D, GP, A, D1)], first=True)
        elif part == 2:
            ag_done(N1M)
            ag_done(C1M)
            mirror_wait(U1)
            add_terms([(N2D, C2D, GP, A, D2), (N1M, C1M, MG, MA, U1)])
        else:
            ag_done(N2M)
            ag_done(C2M)
            mirror_wait(U2)
            add_terms([(N2M, C2M, MG, MA, U2)], last=True)

    steps = dict(
        stage=stage, row=row, rest=rest, add=add, relayed=relayed, hidden=branch, mirror=mirror_hidden,
        partial=spread, pair=rs_pair, cross=rs_mid, finish=finish,
    )
    put_rows(g_up[0], C1U)
    put_normed(in_up, 0, U1, N1U)
    pl.semaphore_wait(barrier, 6)
    for step, *where in SCHEDULE:
        steps[step](*where)
    for c in pending:
        c.wait_send()

    @pl.loop(0, NT)
    def _(j):
        for c in out_copies(j):
            c.wait()


def backward(*blocks):
    bf16, f32 = jnp.bfloat16, jnp.float32
    dma = pltpu.SemaphoreType.DMA
    vmem = pl.BlockSpec(memory_space=pltpu.VMEM)
    hbm = pl.BlockSpec(memory_space=pl.ANY)
    return pl.pallas_call(
        kernel,
        out_shape=(
            jax.ShapeDtypeStruct((D, HID), bf16),
            jax.ShapeDtypeStruct((HID, D), bf16),
            jax.ShapeDtypeStruct((1, ROWS, D), bf16),
            jax.ShapeDtypeStruct((1, ROWS, D), bf16),
        ),
        in_specs=[vmem] * 5 + [hbm] * 4,
        out_specs=[hbm] * 2 + [vmem] * 2,
        scratch_shapes=[
            pltpu.VMEM((12, 8, PAD, D), bf16),
            pltpu.VMEM((2, D, HID), bf16),
            pltpu.VMEM((2, HID, D), bf16),
            pltpu.VMEM((4, 8 * PAD, HID), bf16),
            pltpu.VMEM((4, 8 * PAD, HID), bf16),
            pltpu.VMEM((4, 8, PAD, D), bf16),
            pltpu.VMEM((4, 5, PAD, D), bf16),
            pltpu.VMEM((4, 4, HALF, D), bf16),
            pltpu.VMEM((4, PAD, D), bf16),
            pltpu.VMEM((4, PAD, D), f32),
            pltpu.VMEM((4, PAD, 128), f32),
            pltpu.VMEM((PAD, D), f32),
            pltpu.VMEM((2, PAD, D), bf16),
            pltpu.VMEM((2, 8 * PAD, HID), bf16),
            pltpu.VMEM((2, 8 * PAD, HID), bf16),
            pltpu.VMEM((D, HID), f32),
            pltpu.VMEM((HID, D), f32),
            pltpu.VMEM((D, HID), bf16),
            pltpu.VMEM((HID, D), bf16),
            dma((4,)), dma((2, NT)),
            dma((12, 9)), dma((12, 9)),
            dma((4, 9)), dma((4, 9)),
            dma((2,)), dma((2,)),
            dma((4,)), dma((4,)),
            dma((2,)), dma((2,)), dma((2,)), dma((2,)),
        ],
        compiler_params=pltpu.CompilerParams(
            collective_id=0, has_side_effects=True, vmem_limit_bytes=58 * 2**20
        ),
        cost_estimate=pl.CostEstimate(flops=11 * 10**9, bytes_accessed=13 * 10**6, transcendentals=10**6),
        name="relay_backward",
    )(*blocks)


def body(
    inputs_down, inputs_up, grads_down, grads_up, loss_grads,
    first_down, second_down, first_up, second_up, momentum_first, momentum_second,
):
    total_first, total_second, passed_down, passed_up = backward(
        jnp.swapaxes(inputs_down[0], 0, 1), jnp.swapaxes(inputs_up[0], 0, 1), grads_down, grads_up,
        jnp.swapaxes(loss_grads, 0, 1), first_down, second_down, first_up, second_up,
    )
    new = []
    for weight, momentum, total in (
        (first_down, momentum_first, total_first), (second_down, momentum_second, total_second)
    ):
        moment = momentum_decay * momentum.astype(jnp.float32) + total[None].astype(jnp.float32)
        new.append(((weight.astype(jnp.float32) - learning_rate * moment).astype(jnp.bfloat16), moment.astype(jnp.bfloat16)))
    return (new[0][0], new[1][0], new[0][1], new[1][1], passed_down, passed_up)


def solution(mesh):
    placed = (
        P("section", None, "tensor", None),
        P("section", None, "tensor", None),
        P("section", "tensor", None),
        P("section", "tensor", None),
        P(None, "tensor", None),
        P("section", None, "tensor"),
        P("section", "tensor", None),
        P("section", None, "tensor"),
        P("section", "tensor", None),
        P("section", None, "tensor"),
        P("section", "tensor", None),
    )
    return jax.shard_map(
        body,
        mesh=mesh,
        in_specs=placed,
        out_specs=(
            P("section", None, "tensor"),
            P("section", "tensor", None),
            P("section", None, "tensor"),
            P("section", "tensor", None),
            P("section", "tensor", None),
            P("section", "tensor", None),
        ),
        check_vma=False,
    )
```

```python
import functools

import jax
import jax.numpy as jnp
from jax import lax
from jax.experimental import pallas as pl
from jax.experimental.pallas import tpu as pltpu
from jax.sharding import PartitionSpec as P

D = 2048
FF = 4096
ROWS = 30
PAD = 32
HID = 512
TILE = 256
MESH = pl.DeviceIdType.MESH

epsilon = 1e-05
learning_rate = 0.25
momentum_decay = 0.9
tanh_scale = 0.7978845608028654
cubic_term = 0.044715

N1U, C1U, N2U, C2U, N1D, C1D, N2D, C2D, N1M, C1M, N2M, C2M = range(12)
U1, U2, D1, D2 = range(4)
NT = D // TILE
HALF = PAD // 2
MODES = (1, 0, 0, 0, 0, 1, 0, 0, 0, 0, 1, 0)
SCHEDULE = (
    ("stage", C1U, 0), ("row", C1U), ("stage", N1U, 0), ("rest",), ("row", N1U), ("stage", N1D, 0),
    ("stage", N1U, 1), ("stage", C1U, 1), ("stage", N1U, 2), ("stage", C1D, 0), ("stage", C1U, 2),
    ("stage", N2D, 0), ("stage", C1D, 1), ("stage", N1D, 1), ("stage", C1M, 0), ("hidden", U1),
    ("stage", C1D, 2), ("stage", N1D, 2), ("pair", U1), ("stage", N1M, 0), ("stage", N2U, 0), ("cross", U1),
    ("row", N2U), ("stage", C1M, 1), ("hidden", D1), ("stage", N1M, 1), ("finish", U1), ("pair", D1),
    ("stage", N2U, 1), ("add", 1), ("relayed", 0), ("stage", C2U, 0), ("cross", D1), ("row", C2U),
    ("stage", N2M, 0), ("stage", N2D, 1), ("stage", C2U, 1), ("stage", N2U, 2), ("finish", D1),
    ("stage", C2M, 0), ("relayed", 1), ("stage", C2D, 0), ("mirror", U1), ("stage", C2U, 2), ("stage", C2M, 1),
    ("stage", C2D, 1), ("stage", N2D, 2), ("stage", C1M, 2), ("hidden", U2), ("partial", U2), ("mirror", U2),
    ("stage", C2D, 2), ("stage", N1M, 2), ("pair", U2), ("stage", N2M, 1), ("hidden", D2), ("stage", C2M, 2),
    ("add", 2), ("cross", U2), ("stage", N2M, 2), ("pair", D2), ("cross", D2), ("finish", U2), ("add", 3),
    ("finish", D2),
)


def gelu_with_slope(preact):
    tanh_input = tanh_scale * (preact + cubic_term * preact * preact * preact)
    tangent = jnp.tanh(tanh_input)
    values = 0.5 * preact * (1.0 + tangent)
    slopes = 0.5 * (1.0 + tangent) + 0.5 * preact * (1.0 - tangent * tangent) * tanh_scale * (
        1.0 + 3.0 * cubic_term * preact * preact
    )
    return (values, slopes)


def dot_nt(a, b):
    return lax.dot_general(a, b, (((1,), (1,)), ((), ())), preferred_element_type=jnp.float32)


def dot_tn(a, b):
    return lax.dot_general(a, b, (((0,), (0,)), ((), ())), preferred_element_type=jnp.float32)


def kernel(
    in_down, in_up, g_down, g_up, loss, w1d_h, w2d_h, w1u_h, w2u_h,
    t1_h, t2_h, pass_d, pass_u,
    G, W1, W2, A, GP, PB, RR, RH, ZB, NR, SC, CT, RL, MG, MA, ACC1, ACC2, T1, T2,
    load_sem, out_sem, ag_s, ag_r, rs_s, rs_r, rl_s, rl_r, row_s, row_r, mg_s, mg_r, ma_s, ma_r,
):
    s = lax.axis_index("section")
    t = lax.axis_index("tensor")
    x = lax.rem(t, 4)
    zh = t // 4
    zo = 1 - zh

    def xpeer(k):
        return (s, zh * 4 + lax.rem(x + k, 4))

    zpeer = (s, zo * 4 + x)
    mirror = (15 - s, t)
    up = (lax.rem(s + 1, 16), t)
    down = (lax.rem(s + 15, 16), t)

    barrier = pltpu.get_barrier_semaphore()
    for peer in (xpeer(1), xpeer(3), zpeer, mirror, up, down):
        pl.semaphore_signal(barrier, inc=1, device_id=peer, device_id_type=MESH)

    loads = []
    for i, (src, dst) in enumerate(
        ((w1u_h, W1.at[0]), (w2u_h, W2.at[0]), (w1d_h, W1.at[1]), (w2d_h, W2.at[1]))
    ):
        c = pltpu.make_async_copy(src.at[0], dst, load_sem.at[i])
        c.start()
        loads.append(c)

    def put_normed(ref, step, q, a):
        wide = ref[...].astype(jnp.float32)[:, step]
        centred = wide - jnp.mean(wide, axis=-1, keepdims=True)
        inv = lax.rsqrt(jnp.mean(centred * centred, axis=-1, keepdims=True) + epsilon)
        NR[q, ROWS:PAD] = jnp.zeros((PAD - ROWS, D), jnp.float32)
        NR[q, 0:ROWS] = centred * inv
        SC[q, ROWS:PAD] = jnp.zeros((PAD - ROWS, 128), jnp.float32)
        SC[q, 0:ROWS] = jnp.broadcast_to(inv, (ROWS, 128))
        G[a, t] = NR[q].astype(jnp.bfloat16)

    def put_rows(value, a):
        CT[ROWS:PAD] = jnp.zeros((PAD - ROWS, D), jnp.float32)
        CT[0:ROWS] = value.astype(jnp.float32)
        G[a, t] = CT[...].astype(jnp.bfloat16)

    def rcopy(src, dst, ss, rs, dev):
        return pltpu.make_async_remote_copy(
            src_ref=src, dst_ref=dst, send_sem=ss, recv_sem=rs, device_id=dev, device_id_type=MESH
        )

    pending = []

    def send(src, dst, ss, rs, dev):
        c = rcopy(src, dst, ss, rs, dev)
        c.start()
        pending.append(c)

    waited = set()

    def ag_ref(a, slot, half=None):
        return G.at[a, slot] if half is None else G.at[a, slot, pl.ds(half * HALF, HALF)]

    def ag_send(a, i, dev, slot, half=None):
        ref = ag_ref(a, slot, half)
        send(ref, ref, ag_s.at[a, i], ag_r.at[a, i], dev)

    def near(k):
        return zh * 4 + lax.rem(x + k, 4)

    def far(k):
        return zo * 4 + lax.rem(x + k, 4)

    def landing(a, i):
        first = MODES[a] == 0
        return (
            (far(0), None), (near(3), None), (near(1), None), (near(2), 0), (near(2), 1),
            (far(3), None), (far(1), None),
            (far(2), 0 if first else None), (far(2), 1),
        )[i]

    def ag_wait(a, *which):
        for i in which:
            if (a, i) not in waited:
                waited.add((a, i))
                ref = ag_ref(a, *landing(a, i))
                rcopy(ref, ref, ag_s.at[a, i], ag_r.at[a, i], zpeer).wait_recv()

    def ag_done(a):
        ag_wait(a, *range(9 if MODES[a] == 0 else 8))

    def row_wait(i):
        ref = G.at[N1M + i, t]
        rcopy(ref, ref, row_s.at[i], row_r.at[i], mirror).wait_recv()

    def stage(a, k):
        first = MODES[a] == 0
        if k == 0:
            if a >= N1M:
                row_wait(a - N1M)
            if first:
                ag_send(a, 0, zpeer, t)
            ag_send(a, 1, xpeer(1), t)
            ag_send(a, 2, xpeer(3), t)
            if not first:
                ag_send(a, 0, zpeer, t)
        elif k == 1:
            ag_wait(a, 1)
            ag_send(a, 3, xpeer(1), near(3), 0)
            if not first:
                ag_send(a, 5, zpeer, near(3))
            ag_wait(a, 2)
            ag_send(a, 4, xpeer(3), near(1), 1)
            if not first:
                ag_send(a, 6, zpeer, near(1))
            else:
                ag_wait(a, 0)
                ag_send(a, 5, xpeer(1), far(0))
                ag_send(a, 6, xpeer(3), far(0))
        elif first:
            ag_wait(a, 5)
            ag_send(a, 7, xpeer(1), far(3), 0)
            ag_wait(a, 6)
            ag_send(a, 8, xpeer(3), far(1), 1)
        else:
            ag_wait(a, 3, 4)
            ag_send(a, 7, zpeer, near(2))

    def row(a):
        send(G.at[a, t], G.at[N1M + a, t], row_s.at[a], row_r.at[a], mirror)

    def hidden(q, w, an, ac):
        @pl.loop(0, HID // TILE)
        def _(j):
            cols = pl.ds(pl.multiple_of(j * TILE, TILE), TILE)
            n = G[an].reshape(8 * PAD, D)
            pre = jnp.dot(n, W1[w, :, cols], preferred_element_type=jnp.float32) * D ** (-0.5)
            values, slopes = gelu_with_slope(pre)
            A[q, :, cols] = values.astype(jnp.bfloat16)
            c = G[ac].reshape(8 * PAD, D)
            ga = dot_nt(c, W2[w, cols, :]) * FF ** (-0.5)
            GP[q, :, cols] = (ga * slopes).astype(jnp.bfloat16)

    def partial(q, w):
        @pl.loop(0, NT)
        def _(j):
            cols = pl.ds(pl.multiple_of(j * TILE, TILE), TILE)
            part = dot_nt(GP[q], W1[w, cols, :]) * D ** (-0.5)
            PB[q, :, :, cols] = part.astype(jnp.bfloat16).reshape(8, PAD, TILE)

    def rs_send(q, i, src, dst, dev):
        send(src, dst, rs_s.at[q, i], rs_r.at[q, i], dev)

    def rs_start(q):
        for i, block in ((0, far(2)), (2, near(2))):
            rs_send(q, 5 + i, PB.at[q, block, pl.ds(0, HALF)], RH.at[q, i], xpeer(1))
            rs_send(q, 6 + i, PB.at[q, block, pl.ds(HALF, HALF)], RH.at[q, i + 1], xpeer(3))

    def rs_wait(q, i):
        ref = RR.at[q, i] if i < 5 else RH.at[q, i - 5]
        rcopy(ref, ref, rs_s.at[q, i], rs_r.at[q, i], zpeer).wait_recv()

    def rs_pair(q):
        for i, place in ((0, far), (2, near)):
            for k, half in ((1, 0), (3, 1)):
                rs_wait(q, 5 + i + half)
                rows = pl.ds(half * HALF, HALF)
                both = PB[q, place(k), rows].astype(jnp.float32) + RH[q, i + half].astype(jnp.float32)
                PB[q, place(k), rows] = both.astype(jnp.bfloat16)
                rs_send(q, 1 + i + half, PB.at[q, place(k)], RR.at[q, 1 + i + half], xpeer(k))

    def rs_mid(q):
        rs_wait(q, 1)
        rs_wait(q, 2)
        total = PB[q, far(0)].astype(jnp.float32) + RR[q, 1].astype(jnp.float32) + RR[q, 2].astype(jnp.float32)
        ZB[q] = total.astype(jnp.bfloat16)
        rs_send(q, 0, ZB.at[q], RR.at[q, 0], zpeer)

    def rs_end(q, ac):
        rs_wait(q, 3)
        rs_wait(q, 4)
        total = PB[q, t].astype(jnp.float32) + RR[q, 3].astype(jnp.float32) + RR[q, 4].astype(jnp.float32)
        rs_wait(q, 0)
        gn = total + RR[q, 0].astype(jnp.float32)
        normed = NR[q]
        first_mean = jnp.mean(gn, axis=-1, keepdims=True)
        second_mean = jnp.mean(gn * normed, axis=-1, keepdims=True)
        return G[ac, t].astype(jnp.float32) + SC[q, :, 0:1] * (gn - first_mean - normed * second_mean)

    def relay(q, ac, i, a, dev):
        RL[i] = rs_end(q, ac).astype(jnp.bfloat16)
        send(RL.at[i], G.at[a, t], rl_s.at[i], rl_r.at[i], dev)

    def relay_wait(i, a, edge, which):
        rcopy(RL.at[i], G.at[a, t], rl_s.at[i], rl_r.at[i], zpeer).wait_recv()

        @pl.when(s == edge)
        def _():
            put_rows(loss[...].astype(jnp.float32)[:, which], a)

    def mirror_hidden(q):
        send(GP.at[q], MG.at[q], mg_s.at[q], mg_r.at[q], mirror)
        send(A.at[q], MA.at[q], ma_s.at[q], ma_r.at[q], mirror)

    def mirror_wait(q):
        rcopy(GP.at[q], MG.at[q], mg_s.at[q], mg_r.at[q], mirror).wait_recv()
        rcopy(A.at[q], MA.at[q], ma_s.at[q], ma_r.at[q], mirror).wait_recv()

    def flat(a, cols):
        return G[a, :, :, cols].reshape(8 * PAD, TILE)

    def out_copies(j):
        cols = pl.ds(pl.multiple_of(j * TILE, TILE), TILE)
        return (
            pltpu.make_async_copy(T1.at[cols, :], t1_h.at[cols, :], out_sem.at[0, j]),
            pltpu.make_async_copy(T2.at[:, cols], t2_h.at[:, cols], out_sem.at[1, j]),
        )

    def add_terms(terms, first=False, last=False):
        @pl.loop(0, NT)
        def _(j):
            cols = pl.ds(pl.multiple_of(j * TILE, TILE), TILE)
            one = sum(dot_tn(flat(n, cols), gp[q]) for n, c, gp, ac, q in terms)
            two = sum(dot_tn(ac[q], flat(c, cols)) for n, c, gp, ac, q in terms)
            if not first:
                one = one + ACC1[cols, :]
                two = two + ACC2[:, cols]
            if last:
                T1[cols, :] = (one * D ** (-0.5)).astype(jnp.bfloat16)
                T2[:, cols] = (two * FF ** (-0.5)).astype(jnp.bfloat16)
                for c in out_copies(j):
                    c.start()
            else:
                ACC1[cols, :] = one
                ACC2[:, cols] = two

    sources = {U1: (0, N1U, C1U), U2: (0, N2U, C2U), D1: (1, N1D, C1D), D2: (1, N2D, C2D)}

    def branch(q):
        w, an, ac = sources[q]
        for i in (2 * w, 2 * w + 1):
            if i not in waited:
                waited.add(i)
                loads[i].wait()
        ag_done(an)
        ag_done(ac)
        hidden(q, w, an, ac)
        if q != U2:
            spread(q)

    def spread(q):
        partial(q, sources[q][0])
        rs_start(q)

    def finish(q):
        if q == U1:
            relay(q, C1U, 0, C2U, up)
        elif q == D1:
            relay(q, C1D, 1, C2D, down)
        else:
            CT[...] = rs_end(q, sources[q][2])
            (pass_u if q == U2 else pass_d)[0] = CT[0:ROWS].astype(jnp.bfloat16)

    def relayed(i):
        if i == 0:
            relay_wait(0, C2U, 0, 1)
        else:
            relay_wait(1, C2D, 15, 0)

    def rest():
        put_normed(in_down, 0, D1, N1D)
        put_rows(g_down[0], C1D)
        put_normed(in_up, 1, U2, N2U)
        put_normed(in_down, 1, D2, N2D)

    def add(part):
        if part == 1:
            add_terms([(N1D, C1D, GP, A, D1)], first=True)
        elif part == 2:
            ag_done(N1M)
            ag_done(C1M)
            mirror_wait(U1)
            add_terms([(N2D, C2D, GP, A, D2), (N1M, C1M, MG, MA, U1)])
        else:
            ag_done(N2M)
            ag_done(C2M)
            mirror_wait(U2)
            add_terms([(N2M, C2M, MG, MA, U2)], last=True)

    steps = dict(
        stage=stage, row=row, rest=rest, add=add, relayed=relayed, hidden=branch, mirror=mirror_hidden,
        partial=spread, pair=rs_pair, cross=rs_mid, finish=finish,
    )
    put_rows(g_up[0], C1U)
    put_normed(in_up, 0, U1, N1U)
    pl.semaphore_wait(barrier, 6)
    for step, *where in SCHEDULE:
        steps[step](*where)
    for c in pending:
        c.wait_send()

    @pl.loop(0, NT)
    def _(j):
        for c in out_copies(j):
            c.wait()


def backward(*blocks):
    bf16, f32 = jnp.bfloat16, jnp.float32
    dma = pltpu.SemaphoreType.DMA
    vmem = pl.BlockSpec(memory_space=pltpu.VMEM)
    hbm = pl.BlockSpec(memory_space=pl.ANY)
    return pl.pallas_call(
        kernel,
        out_shape=(
            jax.ShapeDtypeStruct((D, HID), bf16),
            jax.ShapeDtypeStruct((HID, D), bf16),
            jax.ShapeDtypeStruct((1, ROWS, D), bf16),
            jax.ShapeDtypeStruct((1, ROWS, D), bf16),
        ),
        in_specs=[vmem] * 5 + [hbm] * 4,
        out_specs=[hbm] * 2 + [vmem] * 2,
        scratch_shapes=[
            pltpu.VMEM((12, 8, PAD, D), bf16),
            pltpu.VMEM((2, D, HID), bf16),
            pltpu.VMEM((2, HID, D), bf16),
            pltpu.VMEM((4, 8 * PAD, HID), bf16),
            pltpu.VMEM((4, 8 * PAD, HID), bf16),
            pltpu.VMEM((4, 8, PAD, D), bf16),
            pltpu.VMEM((4, 5, PAD, D), bf16),
            pltpu.VMEM((4, 4, HALF, D), bf16),
            pltpu.VMEM((4, PAD, D), bf16),
            pltpu.VMEM((4, PAD, D), f32),
            pltpu.VMEM((4, PAD, 128), f32),
            pltpu.VMEM((PAD, D), f32),
            pltpu.VMEM((2, PAD, D), bf16),
            pltpu.VMEM((2, 8 * PAD, HID), bf16),
            pltpu.VMEM((2, 8 * PAD, HID), bf16),
            pltpu.VMEM((D, HID), f32),
            pltpu.VMEM((HID, D), f32),
            pltpu.VMEM((D, HID), bf16),
            pltpu.VMEM((HID, D), bf16),
            dma((4,)), dma((2, NT)),
            dma((12, 9)), dma((12, 9)),
            dma((4, 9)), dma((4, 9)),
            dma((2,)), dma((2,)),
            dma((4,)), dma((4,)),
            dma((2,)), dma((2,)), dma((2,)), dma((2,)),
        ],
        compiler_params=pltpu.CompilerParams(
            collective_id=0, has_side_effects=True, vmem_limit_bytes=58 * 2**20
        ),
        cost_estimate=pl.CostEstimate(flops=11 * 10**9, bytes_accessed=13 * 10**6, transcendentals=10**6),
        name="relay_backward",
    )(*blocks)


def body(
    inputs_down, inputs_up, grads_down, grads_up, loss_grads,
    first_down, second_down, first_up, second_up, momentum_first, momentum_second,
):
    total_first, total_second, passed_down, passed_up = backward(
        jnp.swapaxes(inputs_down[0], 0, 1), jnp.swapaxes(inputs_up[0], 0, 1), grads_down, grads_up,
        jnp.swapaxes(loss_grads, 0, 1), first_down, second_down, first_up, second_up,
    )
    new = []
    for weight, momentum, total in (
        (first_down, momentum_first, total_first), (second_down, momentum_second, total_second)
    ):
        moment = momentum_decay * momentum.astype(jnp.float32) + total[None].astype(jnp.float32)
        new.append(((weight.astype(jnp.float32) - learning_rate * moment).astype(jnp.bfloat16), moment.astype(jnp.bfloat16)))
    return (new[0][0], new[1][0], new[0][1], new[1][1], passed_down, passed_up)


def solution(mesh):
    placed = (
        P("section", None, "tensor", None),
        P("section", None, "tensor", None),
        P("section", "tensor", None),
        P("section", "tensor", None),
        P(None, "tensor", None),
        P("section", None, "tensor"),
        P("section", "tensor", None),
        P("section", None, "tensor"),
        P("section", "tensor", None),
        P("section", None, "tensor"),
        P("section", "tensor", None),
    )
    return jax.shard_map(
        body,
        mesh=mesh,
        in_specs=placed,
        out_specs=(
            P("section", None, "tensor"),
            P("section", "tensor", None),
            P("section", None, "tensor"),
            P("section", "tensor", None),
            P("section", "tensor", None),
            P("section", "tensor", None),
        ),
        check_vma=False,
    )
```
